256 devices in a mesh: outer: 16 (over x, y), inner: 16 (over z, core).
Axes of the slice: x: 4, y: 4, z: 8, core: 2. Of those that a mesh axis runs over, the one named last changes fastest.
Arguments:
- queries: bfloat16 [1, 32768, 512], P(None, ('outer', 'inner')), may hold values from -70 to 70
- keys_values: bfloat16 [1, 32768, 1024], P(None, ('outer', 'inner')), may hold values from -4 to 4
- cotangent: bfloat16 [1, 32768, 512], P(None, ('outer', 'inner')), may hold values from -6 to 6
Outputs:
- attended: bfloat16 [1, 32768, 512], P(None, ('outer', 'inner'))
- query_grad: bfloat16 [1, 32768, 512], P(None, ('outer', 'inner'))
- kv_grad: bfloat16 [1, 32768, 1024], P(None, ('outer', 'inner'))
The draws below stay inside these ranges and needn't reach their ends.
All inputs are finite; a program needn't handle non-finite values.
Results may differ from the reference program's by a relative error of at most 0.012.
The reference program's roundings to bfloat16 on the way (of `summary`, `keyset`, `rounded` and `dscores`) count: a program that leaves them out, or rounds other values in their place, can miss the bound.
Values may be sent and summed in bfloat16 or wider, within the bound.
No kernel may reach another device: no remote copies, remote signals or barrier semaphores. Data moves between devices by JAX's collectives and lax.ppermute only.
A program may use at most 128 MiB of HBM per device.

```python
import math
import jax
import jax.numpy as jnp
from jax import lax

SEQS = 1
LEAF = 128
HEAD_DIM = 64
D = 512
LOG_INNER = 4
LOG_OUTER = 4
TOKENS = 32768


def draw_keys_values(key, part):
    key = jax.random.fold_in(key, 3)
    values = jnp.clip(jax.random.normal(jax.random.fold_in(key, 2), (SEQS, TOKENS, 2 * D), jnp.float32), -4.0, 4.0)
    return values.astype(jnp.bfloat16)


def draw_queries(key, part):
    key = jax.random.fold_in(key, 4)
    values = 2.5 * jnp.clip(jax.random.normal(jax.random.fold_in(key, 3), (SEQS, TOKENS, D), jnp.float32), -4.0, 4.0)
    return values.astype(jnp.bfloat16)


def shard_levels(rng, dims, pieces, low, top_value):
    level = 1.0
    for axis_at, blocks in pieces:
        steps = jax.random.uniform(jax.random.fold_in(jax.random.fold_in(rng, 6), axis_at), (blocks,), jnp.float32, low / len(pieces), top_value / len(pieces))
        level = level * jnp.repeat(jnp.exp(steps), dims[axis_at] // blocks).reshape((-1,) + (1,) * (len(dims) - 1 - axis_at))
    return level


def centred(own_key, shape, scale, most, shards=(), held_as=jnp.bfloat16):
    array = jax.random.normal(own_key, shape, jnp.float32) * scale
    if len(shards) > 0:
        array = shard_levels(own_key, shape, shards, -0.22, 0.18) * array
    return jnp.clip(array, min=-most, max=most).astype(held_as)


def setup_inputs(seed: int = 0) -> dict:
    key_list = jax.random.split(jax.random.key(seed), 4)
    return {
        "queries": draw_queries(jax.random.fold_in(key_list[3], 71), 0),
        "keys_values": draw_keys_values(jax.random.fold_in(key_list[3], 71), 0),
        "cotangent": centred(key_list[2], (SEQS, TOKENS, D), 1.0, 6.0, ((1, 256),)),
    }


HALF_ROOT = 1.0 / math.sqrt(2.0)

def coarsen(summary):
    seq_count, row_count, feature_count = summary.shape
    paired = summary.reshape(seq_count, row_count // 2, 2, feature_count).astype(jnp.float32)
    return (lax.optimization_barrier(jnp.sum(paired, axis=2)) * HALF_ROOT).astype(jnp.bfloat16)

def attend(queries, keyset, cotangent):
    model_width = queries.shape[-1]
    head_count = model_width // HEAD_DIM
    scaling = 1.0 / math.sqrt(HEAD_DIM)
    outputs, query_parts, key_parts, value_parts = ([], [], [], [])
    for head_index in range(head_count):
        low_col = head_index * HEAD_DIM
        high_col = low_col + HEAD_DIM
        head_query = queries[..., low_col:high_col].astype(jnp.float32)
        head_key = keyset[..., low_col:high_col].astype(jnp.float32)
        head_value = keyset[..., model_width + low_col:model_width + high_col].astype(jnp.float32)
        head_grad = cotangent[..., low_col:high_col].astype(jnp.float32)
        scores = jnp.einsum('sqe,ske->sqk', head_query, head_key) * scaling
        row_max = lax.optimization_barrier(jnp.max(scores, axis=-1, keepdims=True))
        weights = jnp.exp(scores - row_max)
        weights = weights / lax.optimization_barrier(jnp.sum(weights, axis=-1, keepdims=True))
        rounded = lax.optimization_barrier(weights.astype(jnp.bfloat16)).astype(jnp.float32)
        outputs.append(jnp.einsum('sqk,ske->sqe', rounded, head_value))
        dweights = jnp.einsum('sqe,ske->sqk', head_grad, head_value)
        centre = lax.optimization_barrier(jnp.sum(weights * dweights, axis=-1, keepdims=True))
        dscores = lax.optimization_barrier((weights * (dweights - centre)).astype(jnp.bfloat16)).astype(jnp.float32)
        query_parts.append(jnp.einsum('sqk,ske->sqe', dscores, head_key) * scaling)
        key_parts.append(jnp.einsum('sqk,sqe->ske', dscores, head_query) * scaling)
        value_parts.append(jnp.einsum('sqk,sqe->ske', rounded, head_grad))
    attended = jnp.concatenate(outputs, axis=-1).astype(jnp.bfloat16)
    query_grad = jnp.concatenate(query_parts, axis=-1).astype(jnp.bfloat16)
    dkeyset = jnp.concatenate(key_parts + value_parts, axis=-1)
    return (attended, query_grad, dkeyset)

def add_rows(table, addition, offset):
    current = lax.dynamic_slice_in_dim(table, offset, addition.shape[1], 1)
    return lax.dynamic_update_slice_in_dim(table, current + addition, offset, 1)

def reference(queries, keys_values, cotangent):
    levels = LOG_INNER + LOG_OUTER
    blocks = TOKENS // LEAF
    summaries = [keys_values]
    for height in range(1, levels):
        summaries.append(coarsen(summaries[-1]))

    def visit(carry, block_index):
        own_acc, level_accs = carry
        offset = (block_index * LEAF).astype(jnp.int32)
        parts = [lax.dynamic_slice_in_dim(keys_values, offset, LEAF, 1)]
        siblings = []
        for height in range(levels):
            sibling = jnp.bitwise_xor(jnp.right_shift(block_index, height), 1).astype(jnp.int32)
            siblings.append(sibling)
            parts.append(lax.dynamic_slice_in_dim(summaries[height], sibling * LEAF, LEAF, 1))
        keyset = jnp.concatenate(parts, axis=1)
        block_query = lax.dynamic_slice_in_dim(queries, offset, LEAF, 1)
        block_grad = lax.dynamic_slice_in_dim(cotangent, offset, LEAF, 1)
        attended, query_grad, dkeyset = attend(block_query, keyset, block_grad)
        own_acc = add_rows(own_acc, dkeyset[:, :LEAF], offset)
        new_accs = []
        for height in range(levels):
            piece_grad = dkeyset[:, (height + 1) * LEAF:(height + 2) * LEAF]
            new_accs.append(add_rows(level_accs[height], piece_grad, siblings[height] * LEAF))
        return ((own_acc, tuple(new_accs)), (attended, query_grad))
    feature_count = keys_values.shape[-1]
    seq_count = keys_values.shape[0]
    start_own = jnp.zeros((seq_count, TOKENS, feature_count), jnp.float32)
    start_levels = tuple((jnp.zeros((seq_count, TOKENS // 2 ** height, feature_count), jnp.float32) for height in range(levels)))
    (own_acc, level_accs), (out_blocks, grad_blocks) = lax.scan(visit, (start_own, start_levels), jnp.arange(blocks, dtype=jnp.int32))
    gradient = own_acc
    for height in range(levels):
        gradient = gradient + jnp.repeat(level_accs[height], 2 ** height, axis=1) * HALF_ROOT ** height
    model_width = queries.shape[-1]
    attended = jnp.swapaxes(out_blocks, 0, 1).reshape(seq_count, TOKENS, model_width)
    query_grad = jnp.swapaxes(grad_blocks, 0, 1).reshape(seq_count, TOKENS, model_width)
    return (attended, query_grad, gradient.astype(jnp.bfloat16))
```

```python
import functools
import math

import jax
import jax.numpy as jnp
from jax import lax
from jax.experimental import pallas as pl
from jax.experimental.pallas import tpu as pltpu
from jax.sharding import PartitionSpec as P

LEAF = 128
D = 512
HALF = 256
HEAD_DIM = 64
FIRST = 640
SECOND = 512
HALF_ROOT = 1.0 / math.sqrt(2.0)
SCALE = 1.0 / math.sqrt(HEAD_DIM)
BF16 = jnp.bfloat16
F32 = jnp.float32
VMEM = pl.BlockSpec(memory_space=pltpu.VMEM)
ANYWHERE = pl.BlockSpec(memory_space=pl.ANY)


def call(body, name, outs, scratch=(), flops=0, spec=VMEM, after=()):
    def run(*operands):
        count = len(operands)
        operands = (*operands, *after)
        shapes = [jax.ShapeDtypeStruct(shape, dtype) for shape, dtype in outs]
        moved = sum(math.prod(s.shape) * s.dtype.itemsize for s in (*operands, *shapes))
        return pl.pallas_call(
            (lambda *refs: body(*refs[:count], *refs[count + len(after) :])),
            out_shape=shapes,
            in_specs=[spec] * count + [ANYWHERE] * len(after),
            out_specs=[VMEM] * len(shapes),
            scratch_shapes=list(scratch),
            name=name,
            cost_estimate=pl.CostEstimate(flops=flops, bytes_accessed=moved, transcendentals=0),
            compiler_params=pltpu.CompilerParams(vmem_limit_bytes=24 * 1024 * 1024),
        )(*operands)

    return run


def exchange(array, partner):
    return lax.ppermute(array, "inner", [(i, partner(i)) for i in range(16)])


def across_cores(i):
    return i ^ 1


def along_z(bits):
    return lambda i: i ^ (bits << 1)


def odd_links(i):
    z, core = i >> 1, i & 1
    z = (z + 1) % 8 if z & 1 else (z - 1) % 8
    return z << 1 | core


def columns(start, core, width=HALF):
    return pl.ds(pl.multiple_of(start + HALF * core, 128), width)


def this_core():
    return lax.axis_index("inner") & 1


def class_of(k):
    return k.bit_length() - 1


def row_index():
    return lax.broadcasted_iota(jnp.int32, (16, D), 0)


def read_rows(ref, count, first=0, step=1):
    return jnp.concatenate([ref[c, pl.ds(first, count, stride=step), :] for c in range(ref.shape[0])], axis=1)


def write_rows(ref, rows, first=0, step=1):
    for c in range(ref.shape[0]):
        ref[c, pl.ds(first, rows.shape[0], stride=step), :] = rows[:, 128 * c : 128 * c + 128]


def halve(rows, apart):
    pooled = (rows + pltpu.roll(rows, 16 - apart, 0)) * HALF_ROOT
    return pooled.astype(BF16).astype(F32)


def half_columns(ref, core):
    return jnp.concatenate([ref[:, columns(0, core)], ref[:, columns(D, core)]], axis=1)


def own_half_kernel(kv_ref, out_ref):
    out_ref[...] = half_columns(kv_ref, this_core())


def pool_kernel(own_ref, sib_ref, slots_ref, one_ref, two_ref, three_ref, tokens_ref, rows_ref):
    tokens = jnp.concatenate([own_ref[...], half_columns(sib_ref, this_core())], axis=0)
    tokens_ref[...] = tokens
    write_rows(rows_ref, tokens.astype(F32))
    count = 2 * LEAF
    for out_ref in (one_ref, two_ref, three_ref, None):
        count //= 2
        pooled = ((read_rows(rows_ref, count, 0, 2) + read_rows(rows_ref, count, 1, 2)) * HALF_ROOT).astype(BF16)
        if out_ref is not None:
            out_ref[...] = pooled
            write_rows(rows_ref, pooled.astype(F32))
    four = pooled.astype(F32)
    outer = lax.axis_index("outer")
    row = row_index()
    five = halve(four, 1)
    six = halve(five, 2)
    seven = halve(six, 4)
    five = jnp.where(row & 1 == 0, five, pltpu.roll(five, 1, 0))
    six = jnp.where(row & 3 == 0, six, 0.0)
    seven = jnp.where(row & 7 == 0, seven, 0.0)
    for by in (1, 2):
        six = six + pltpu.roll(six, by, 0)
    for by in (1, 2, 4):
        seven = seven + pltpu.roll(seven, by, 0)
    table = [
        four,
        jnp.where(row & 1 == outer & 1, five, 0.0),
        jnp.where(row & 3 == outer & 3, six, 0.0),
        jnp.where(row & 7 == outer & 7, seven, 0.0),
    ]
    table = [rows.astype(BF16) for rows in table]
    slots_ref[outer] = jnp.zeros_like(table[0])
    for k in range(1, 16):
        slots_ref[outer ^ k] = table[class_of(k)]


def class_sums(slots_ref):
    outer = lax.axis_index("outer")
    sums = []
    for c in range(4):
        parts = [slots_ref[outer ^ k].astype(F32) for k in range(1 << c, 2 << c)]
        sums.append(functools.reduce(jnp.add, parts))
    return sums


def collect_kernel(slots_ref, three_ref, far_ref):
    far_ref[:64, :] = jnp.concatenate(class_sums(slots_ref), axis=0).astype(BF16)
    far_ref[64:, :] = three_ref[...]


def near_kernel(far_ref, two_ref, near_ref):
    near_ref[:64, :] = far_ref[:64, :]
    near_ref[64:, :] = two_ref[...]


def join_kernel(far_ref, got2_ref, got4_ref, got6_ref, one_ref, upper_ref, lower_ref):
    upper_ref[0:64, :] = far_ref[0:64, :]
    upper_ref[64:128, :] = got2_ref[0:64, :]
    upper_ref[128:192, :] = got4_ref[0:64, :]
    upper_ref[192:256, :] = got6_ref[0:64, :]
    lower_ref[0:128, :] = one_ref[...]
    lower_ref[128:192, :] = got2_ref[64:128, :]
    lower_ref[192:224, :] = got4_ref[64:96, :]
    lower_ref[224:256, :] = got6_ref[64:96, :]


def across(a, b):
    return lax.dot_general(a, b, (((1,), (1,)), ((), ())), preferred_element_type=F32)


def along(a, b):
    return lax.dot_general(a, b, (((0,), (0,)), ((), ())), preferred_element_type=F32)


def two_heads(ref, sib_ref, p, core, factor):
    cols = columns(128 * p, core, 128)
    block = jnp.concatenate([ref[:, cols], sib_ref[:, cols]], axis=0).astype(F32) * factor
    low_half = lax.broadcasted_iota(jnp.int32, block.shape, 1) < HEAD_DIM
    return jnp.concatenate([jnp.where(low_half, block, 0.0), jnp.where(low_half, 0.0, block)], axis=0).astype(BF16)


def pair_columns(p):
    return slice(128 * p, 128 * p + 128), slice(HALF + 128 * p, HALF + 128 * p + 128)


def first_kernel(
    q_ref, qs_ref, cot_ref, cots_ref, tokens_ref, up_ref, low_ref,
    keys_ref, q2_ref, cot2_ref, exps_ref, dweights_ref, max_ref, sum_ref, dot_ref,
):
    core = this_core()
    keys_ref[0:256, :] = tokens_ref[...]
    keys_ref[256:512, :] = up_ref[...]
    keys_ref[512:640, :] = low_ref[128:256, :]
    for p in range(2):
        queries = two_heads(q_ref, qs_ref, p, core, SCALE)
        grads = two_heads(cot_ref, cots_ref, p, core, 1.0)
        q2_ref[p] = queries
        cot2_ref[p] = grads
        key_cols, val_cols = pair_columns(p)
        scores = across(keys_ref[:, key_cols], queries)
        top = jnp.max(scores, axis=0, keepdims=True)
        exps = jnp.exp(scores - top)
        dweights = across(keys_ref[:, val_cols], grads)
        exps_ref[p] = exps
        dweights_ref[p] = dweights
        max_ref[p] = top
        sum_ref[p] = jnp.sum(exps, axis=0, keepdims=True)
        dot_ref[p] = jnp.sum(exps * dweights, axis=0, keepdims=True)


def second_kernel(
    up_ref, low_ref, q2_ref, cot2_ref, max_ref, sum_ref, dot_ref, send_up_ref, send_low_ref, factor_ref, centre_ref, rounded_ref, dscores_ref
):
    for p in range(2):
        queries, grads = q2_ref[p], cot2_ref[p]
        key_cols, val_cols = pair_columns(p)
        scores = across(jnp.concatenate([up_ref[:, key_cols], low_ref[:, key_cols]], axis=0), queries)
        dweights = across(jnp.concatenate([up_ref[:, val_cols], low_ref[:, val_cols]], axis=0), grads)
        top = jnp.maximum(max_ref[p], jnp.max(scores, axis=0, keepdims=True))
        exps = jnp.exp(scores - top)
        before = jnp.exp(max_ref[p] - top)
        inverse = 1.0 / (sum_ref[p] * before + jnp.sum(exps, axis=0, keepdims=True))
        centre = (dot_ref[p] * before + jnp.sum(exps * dweights, axis=0, keepdims=True)) * inverse
        weights = exps * inverse
        rounded = weights.astype(BF16)
        dscores = (weights * (dweights - centre)).astype(BF16)
        factor_ref[p] = before * inverse
        centre_ref[p] = centre
        rounded_ref[p] = rounded
        dscores_ref[p] = dscores
        dkeys = jnp.dot(dscores, queries, preferred_element_type=F32).astype(BF16)
        dvals = jnp.dot(rounded, grads, preferred_element_type=F32).astype(BF16)
        send_up_ref[:, key_cols] = dkeys[:256]
        send_up_ref[:, val_cols] = dvals[:256]
        send_low_ref[:, key_cols] = dkeys[256:]
        send_low_ref[:, val_cols] = dvals[256:]


def rest_kernel(
    keys_ref, up_ref, low_ref, q2_ref, cot2_ref, exps_ref, dweights_ref, factor_ref, centre_ref, rounded_ref, dscores_ref,
    dkeys_ref, mine_ref, swap_ref,
):
    def blocks(pair):
        return [
            jnp.concatenate([pair[:HEAD_DIM, i : i + LEAF], pair[HEAD_DIM:, HALF + i : HALF + i + LEAF]], axis=0).T
            for i in (0, LEAF)
        ]

    for p in range(2):
        key_cols, val_cols = pair_columns(p)
        weights = exps_ref[p] * factor_ref[p]
        rounded = weights.astype(BF16)
        dscores = (weights * (dweights_ref[p] - centre_ref[p])).astype(BF16)
        dkeys_ref[:, key_cols] = jnp.dot(dscores, q2_ref[p], preferred_element_type=F32)
        dkeys_ref[:, val_cols] = jnp.dot(rounded, cot2_ref[p], preferred_element_type=F32)
        later = slice(0, 256), slice(256, 512)
        attended = along(keys_ref[:, val_cols], rounded)
        query_grad = along(keys_ref[:, key_cols], dscores)
        for ref, rows in ((up_ref, later[0]), (low_ref, later[1])):
            attended += along(ref[:, val_cols], rounded_ref[p, rows, :])
            query_grad += along(ref[:, key_cols], dscores_ref[p, rows, :])
        for cols, pair, scale in ((key_cols, attended, 1.0), (val_cols, query_grad, SCALE)):
            for ref, block in zip((mine_ref, swap_ref), blocks(pair), strict=True):
                ref[:, cols] = (block * scale).astype(BF16)


def outputs_kernel(mine_ref, swapped_ref, att_ref, dq_ref, token_ref):
    core = this_core()
    token_ref[...] = jnp.zeros_like(token_ref)
    for ref, start in ((att_ref, 0), (dq_ref, HALF)):
        ref[:, columns(0, core)] = mine_ref[:, start : start + HALF]
        ref[:, columns(0, 1 - core)] = swapped_ref[:, start : start + HALF]


def add(*parts):
    return functools.reduce(jnp.add, [p.astype(F32) for p in parts])


def split_kernel(dkeys_ref, got_up_ref, got_low_ref, own_ref, out2_ref, out4_ref, out6_ref, low2_ref, low6_ref):
    upper = add(dkeys_ref[256:512, :], got_up_ref[...])
    lower = add(dkeys_ref[512:640, :], got_low_ref[128:256, :])
    own_ref[...] = upper[0:64]
    upper, lower = upper.astype(BF16), lower.astype(BF16)
    out2_ref[...] = upper[64:128]
    out4_ref[0:64, :] = upper[128:192]
    out4_ref[64:96, :] = lower[64:96]
    out6_ref[...] = upper[192:256]
    low2_ref[...] = lower[0:64]
    low6_ref[...] = lower[96:128]


def scatter_kernel(own_ref, got2_ref, got4_ref, got6_ref, slots_ref):
    total = add(own_ref[...], got2_ref[...], got4_ref[0:64, :], got6_ref[...]).astype(BF16)
    outer = lax.axis_index("outer")
    slots_ref[outer] = jnp.zeros_like(total[:16])
    for k in range(1, 16):
        c = class_of(k)
        slots_ref[outer ^ k] = total[16 * c : 16 * c + 16]


def finish_kernel(slots_ref, low2_ref, got4_ref, low6_ref, got_low_ref, dkeys_ref, mine_ref, swap_ref, rows_ref):
    outer = lax.axis_index("outer")
    row = row_index()
    four, five, six, seven = class_sums(slots_ref)

    def spread(rows, apart):
        return rows + jnp.where(row & apart == 0, pltpu.roll(rows, 16 - apart, 0), pltpu.roll(rows, apart, 0))

    five = spread(jnp.where(row & 1 == outer & 1, five, 0.0), 1)
    six = spread(spread(jnp.where(row & 3 == outer & 3, six, 0.0), 1), 2)
    seven = spread(spread(spread(jnp.where(row & 7 == outer & 7, seven, 0.0), 1), 2), 4)
    total = four + HALF_ROOT * (five + HALF_ROOT * (six + HALF_ROOT * seven))
    three = add(got4_ref[64:96, :], low6_ref[...])
    two = low2_ref[...].astype(F32)
    one = got_low_ref[0:128, :].astype(F32)
    count = 16
    for level in (three, two, one, dkeys_ref[0:256, :]):
        write_rows(rows_ref, total, 0, 2)
        write_rows(rows_ref, total, 1, 2)
        count *= 2
        total = level + HALF_ROOT * read_rows(rows_ref, count)
    total = total.astype(BF16)
    mine_ref[...] = total[:LEAF]
    swap_ref[...] = total[LEAF:]


def result_kernel(mine_ref, swapped_ref, out_ref):
    core = this_core()
    for start in (0, HALF):
        ref_start = 2 * start
        out_ref[:, columns(ref_start, core)] = mine_ref[:, start : start + HALF]
        out_ref[:, columns(ref_start, 1 - core)] = swapped_ref[:, start : start + HALF]


def shards(queries, keys_values, cotangent):
    queries, keys_values, cotangent = queries[0], keys_values[0], cotangent[0]
    rows = pltpu.VMEM((D // 128, 2 * LEAF, 128), F32)

    def wide(count, dtype=BF16):
        return ((count, D), dtype)

    slots = ((16, 16, D), BF16)

    sibling = exchange(keys_values, across_cores)
    queries_c = exchange(queries, across_cores)
    cotangent_c = exchange(cotangent, across_cores)
    (own,) = call(own_half_kernel, "own_half", [wide(LEAF)])(keys_values)
    sent, one, two, three, tokens = call(pool_kernel, "pool", [slots, wide(128), wide(64), wide(32), wide(256)], [rows])(
        own, sibling
    )
    taken = lax.all_to_all(sent, "outer", 0, 0, tiled=True)
    (far,) = call(collect_kernel, "collect", [wide(96)])(taken, three)
    (near,) = call(near_kernel, "near", [wide(128)])(far, two)
    got4 = exchange(far, along_z(4))
    got6 = exchange(far, along_z(6))
    got2 = exchange(near, along_z(2))
    upper, lower = call(join_kernel, "join", [wide(256), wide(256)])(far, got2, got4, got6, one)
    upper_z = exchange(upper, odd_links)
    lower_z = exchange(lower, along_z(1))

    pairs = ((2, 4 * LEAF, 128), BF16)
    stat = ((2, 1, 4 * LEAF), F32)
    keys, q2, cot2, exps, dweights, top, total, dots = call(
        first_kernel,
        "first",
        [wide(FIRST), pairs, pairs, ((2, FIRST, 4 * LEAF), F32), ((2, FIRST, 4 * LEAF), F32), stat, stat, stat],
        flops=4 * LEAF * FIRST * D,
    )(queries, queries_c, cotangent, cotangent_c, tokens, upper, lower)
    square = ((2, SECOND, 4 * LEAF), BF16)
    back_up, back_low, factor, centre, rounded, dscores = call(
        second_kernel, "second", [wide(256), wide(256), stat, stat, square, square], flops=8 * LEAF * SECOND * D
    )(upper_z, lower_z, q2, cot2, top, total, dots)
    gotz_up = exchange(back_up, odd_links)
    gotz_low = exchange(back_low, along_z(1))
    dkeys, mine, swap = call(
        rest_kernel, "rest", [wide(FIRST, F32), wide(LEAF), wide(LEAF)], flops=8 * LEAF * 1152 * D
    )(keys, upper_z, lower_z, q2, cot2, exps, dweights, factor, centre, rounded, dscores)
    swapped = exchange(swap, across_cores)
    attended, query_grad, token = call(outputs_kernel, "outputs", [wide(LEAF), wide(LEAF), ((8, 128), F32)])(mine, swapped)

    block, out2, out4, out6, low2, low6 = call(
        split_kernel, "split", [wide(64, F32), wide(64), wide(96), wide(64), wide(64), wide(32)], after=(swapped,)
    )(dkeys, gotz_up, gotz_low)
    back4 = exchange(out4, along_z(4))
    back2 = exchange(out2, along_z(2))
    back6 = exchange(out6, along_z(6))
    low2 = exchange(low2, along_z(2))
    low6 = exchange(low6, along_z(6))
    (sent,) = call(scatter_kernel, "scatter", [slots], after=(token,))(block, back2, back4, back6)
    taken = lax.all_to_all(sent, "outer", 0, 0, tiled=True)
    mine, swap = call(finish_kernel, "finish", [wide(LEAF), wide(LEAF)], [rows])(taken, low2, back4, low6, gotz_low, dkeys)
    swapped = exchange(swap, across_cores)
    (kv_grad,) = call(result_kernel, "result", [((LEAF, 2 * D), BF16)])(mine, swapped)
    return attended[None], query_grad[None], kv_grad[None]


def solution(mesh):
    spec = P(None, ("outer", "inner"), None)
    return jax.shard_map(shards, mesh=mesh, in_specs=(spec,) * 3, out_specs=(spec,) * 3, check_vma=False)
```

```python
import functools
import math

import jax
import jax.numpy as jnp
from jax import lax
from jax.experimental import pallas as pl
from jax.experimental.pallas import tpu as pltpu
from jax.sharding import PartitionSpec as P

LEAF = 128
D = 512
TEAM = 4
COLS = 128
HEAD_DIM = 64
HALF_ROOT = 1.0 / math.sqrt(2.0)
SCALE = 1.0 / math.sqrt(HEAD_DIM)
BF16 = jnp.bfloat16
F32 = jnp.float32
VMEM = pl.BlockSpec(memory_space=pltpu.VMEM)


def call(body, name, outs, scratch=(), flops=0):
    def run(*operands):
        shapes = [jax.ShapeDtypeStruct(shape, dtype) for shape, dtype in outs]
        moved = sum(math.prod(s.shape) * s.dtype.itemsize for s in (*operands, *shapes))
        return pl.pallas_call(
            body,
            out_shape=shapes,
            in_specs=[VMEM] * len(operands),
            out_specs=[VMEM] * len(shapes),
            scratch_shapes=list(scratch),
            name=name,
            cost_estimate=pl.CostEstimate(flops=flops, bytes_accessed=moved, transcendentals=0),
            compiler_params=pltpu.CompilerParams(vmem_limit_bytes=24 * 1024 * 1024),
        )(*operands)

    return run


def exchange(array, bits):
    return lax.ppermute(array, "inner", [(i, i ^ bits) for i in range(16)])


def trade_slots(slots):
    groups = [[16 * o + 4 * team + m for o in range(16) for m in range(TEAM)] for team in range(4)]
    return lax.all_to_all(slots, ("outer", "inner"), 0, 0, axis_index_groups=groups, tiled=True)


def member():
    return lax.axis_index("inner") & 3


def columns(start, group):
    return pl.ds(pl.multiple_of(start + COLS * group, COLS), COLS)


def class_of(k):
    return k.bit_length() - 1


def row_index():
    return lax.broadcasted_iota(jnp.int32, (8, 2 * D), 0)


def read_rows(ref, count, first=0, step=1):
    return jnp.concatenate([ref[c, pl.ds(first, count, stride=step), :] for c in range(ref.shape[0])], axis=1)


def write_rows(ref, rows, first=0, step=1):
    for c in range(ref.shape[0]):
        ref[c, pl.ds(first, rows.shape[0], stride=step), :] = rows[:, 128 * c : 128 * c + 128]


def pool_rows(ref, count):
    pooled = ((read_rows(ref, count // 2, 0, 2) + read_rows(ref, count // 2, 1, 2)) * HALF_ROOT).astype(BF16)
    write_rows(ref, pooled.astype(F32))
    return pooled


def halve(rows, apart):
    pooled = (rows + pltpu.roll(rows, 8 - apart, 0)) * HALF_ROOT
    return pooled.astype(BF16).astype(F32)


def spread(rows, apart):
    row = row_index()
    return rows + jnp.where(row & apart == 0, pltpu.roll(rows, 8 - apart, 0), pltpu.roll(rows, apart, 0))


def pool_kernel(kv_ref, slots_ref, own_ref, out1_ref, out2_ref, out3_ref, rows_ref):
    write_rows(rows_ref, kv_ref[...].astype(F32))
    for count in (128, 64, 32, 16):
        four = pool_rows(rows_ref, count)
    four = four.astype(F32)
    outer = lax.axis_index("outer")
    row = row_index()
    five = halve(four, 1)
    six = halve(five, 2)
    seven = halve(six, 4)
    five = jnp.where(row & 1 == 0, five, pltpu.roll(five, 1, 0))
    six = spread(spread(jnp.where(row & 3 == 0, six, 0.0), 1), 2)
    seven = jnp.broadcast_to(seven[:1], seven.shape)
    table = [
        four,
        jnp.where(row & 1 == outer & 1, five, 0.0),
        jnp.where(row & 3 == outer & 3, six, 0.0),
        jnp.where(row == outer & 7, seven, 0.0),
    ]
    for m in range(TEAM):
        keys, values = slice(COLS * m, COLS * m + COLS), slice(D + COLS * m, D + COLS * m + COLS)
        blocks = [jnp.concatenate([rows[:, keys], rows[:, values]], axis=0).astype(BF16) for rows in table]
        slots_ref[outer * TEAM + m] = jnp.zeros_like(blocks[0])
        for k in range(1, 16):
            slots_ref[(outer ^ k) * TEAM + m] = blocks[class_of(k)]
    pack(kv_ref, 0, kv_ref, D, (own_ref, out1_ref, out2_ref, out3_ref))


def pack(left_ref, left, right_ref, right, out_refs):
    for k, ref in enumerate(out_refs):
        ref[:, :COLS] = left_ref[:, columns(left, member() ^ k)]
        ref[:, COLS:] = right_ref[:, columns(right, member() ^ k)]


def pack_kernel(q_ref, cot_ref, *out_refs):
    pack(q_ref, 0, cot_ref, 0, out_refs)


def class_sums(slots_ref):
    outer = lax.axis_index("outer")

    def total(c, m):
        return functools.reduce(jnp.add, [slots_ref[(outer ^ k) * TEAM + m].astype(F32) for k in range(1 << c, 2 << c)])

    return [[total(c, m) for m in range(TEAM)] for c in range(4)]


def side_by_side(block):
    return jnp.concatenate([block[:8], block[8:]], axis=1)


def collect_kernel(slots_ref, own_ref, got1_ref, got2_ref, got3_ref, _, tokens_ref, one_ref, near_ref, far_ref, rows_ref):
    for k, ref in enumerate((own_ref, got1_ref, got2_ref, got3_ref)):
        tokens_ref[LEAF * k : LEAF * k + LEAF, :] = ref[...]
    write_rows(rows_ref, tokens_ref[...].astype(F32))
    one_ref[...] = pool_rows(rows_ref, 512)
    near_ref[128:256, :] = pool_rows(rows_ref, 256)
    far_ref[128:192, :] = pool_rows(rows_ref, 128)
    block = jnp.concatenate([side_by_side(b) for blocks in class_sums(slots_ref) for b in blocks], axis=0).astype(BF16)
    near_ref[0:128, :] = block
    far_ref[0:128, :] = block


def across(a, b):
    return lax.dot_general(a, b, (((1,), (1,)), ((), ())), preferred_element_type=F32)


def along(a, b):
    return lax.dot_general(a, b, (((0,), (0,)), ((), ())), preferred_element_type=F32)


def two_heads(block):
    low_half = lax.broadcasted_iota(jnp.int32, block.shape, 1) < HEAD_DIM
    return jnp.concatenate([jnp.where(low_half, block, 0.0), jnp.where(low_half, 0.0, block)], axis=0).astype(BF16)


def first_kernel(
    own_ref, got1_ref, got2_ref, got3_ref, tokens_ref, one_ref, far_ref, keys_ref, q2_ref, cot2_ref, exps_ref, dweights_ref, max_ref, sum_ref, dot_ref
):
    for s, refs in enumerate(((own_ref, got1_ref), (got2_ref, got3_ref))):
        keys_ref[s, 0:256, :] = tokens_ref[256 * s : 256 * s + 256, :]
        keys_ref[s, 256:384, :] = one_ref[128 - 128 * s : 256 - 128 * s, :]
        keys_ref[s, 384:512, :] = far_ref[0:128, :]
        tokens = jnp.concatenate([ref[...] for ref in refs], axis=0).astype(F32)
        queries = two_heads(tokens[:, :COLS] * SCALE)
        grads = two_heads(tokens[:, COLS:])
        q2_ref[s] = queries
        cot2_ref[s] = grads
        scores = across(keys_ref[s, :, 0:128], queries)
        top = jnp.max(scores, axis=0, keepdims=True)
        exps = jnp.exp(scores - top)
        dweights = across(keys_ref[s, :, 128:256], grads)
        exps_ref[s] = exps
        dweights_ref[s] = dweights
        max_ref[s] = top
        sum_ref[s] = jnp.sum(exps, axis=0, keepdims=True)
        dot_ref[s] = jnp.sum(exps * dweights, axis=0, keepdims=True)


def second_kernel(
    got2_ref, got4_ref, got6_ref, q2_ref, cot2_ref, max_ref, sum_ref, dot_ref,
    send2_ref, send4_ref, send6_ref, keys_ref, factor_ref, centre_ref, rounded_ref, dscores_ref,
):
    keys_ref[0:256, :] = got2_ref[...]
    keys_ref[256:448, :] = got4_ref[...]
    keys_ref[448:640, :] = got6_ref[...]
    dkeys, dvals = [], []
    for s in range(2):
        queries, grads = q2_ref[s], cot2_ref[s]
        scores = across(keys_ref[:, 0:128], queries)
        dweights = across(keys_ref[:, 128:256], grads)
        top = jnp.maximum(max_ref[s], jnp.max(scores, axis=0, keepdims=True))
        exps = jnp.exp(scores - top)
        before = jnp.exp(max_ref[s] - top)
        inverse = 1.0 / (sum_ref[s] * before + jnp.sum(exps, axis=0, keepdims=True))
        centre = (dot_ref[s] * before + jnp.sum(exps * dweights, axis=0, keepdims=True)) * inverse
        weights = exps * inverse
        rounded = weights.astype(BF16)
        dscores = (weights * (dweights - centre)).astype(BF16)
        factor_ref[s] = before * inverse
        centre_ref[s] = centre
        rounded_ref[s] = rounded
        dscores_ref[s] = dscores
        dkeys.append(jnp.dot(dscores, queries, preferred_element_type=F32))
        dvals.append(jnp.dot(rounded, grads, preferred_element_type=F32))
    for cols, parts in ((slice(0, 128), dkeys), (slice(128, 256), dvals)):
        total = (parts[0] + parts[1]).astype(BF16)
        send2_ref[:, cols] = total[0:256]
        send4_ref[:, cols] = total[256:448]
        send6_ref[:, cols] = total[448:640]


def rest_kernel(
    keys_ref, later_ref, q2_ref, cot2_ref, exps_ref, dweights_ref, factor_ref, centre_ref, rounded_ref, dscores_ref,
    block_ref, one_ref, zero_ref, *results_refs,
):
    totals = []
    for s in range(2):
        weights = exps_ref[s] * factor_ref[s]
        rounded = weights.astype(BF16)
        dscores = (weights * (dweights_ref[s] - centre_ref[s])).astype(BF16)
        dkeys = jnp.dot(dscores, q2_ref[s], preferred_element_type=F32)
        dvals = jnp.dot(rounded, cot2_ref[s], preferred_element_type=F32)
        total = jnp.concatenate([dkeys, dvals], axis=1)
        zero_ref[256 * s : 256 * s + 256, :] = total[0:256]
        one_ref[128 - 128 * s : 256 - 128 * s, :] = total[256:384]
        totals.append(total[384:512])
        attended = along(keys_ref[s, :, 128:256], rounded) + along(later_ref[:, 128:256], rounded_ref[s])
        query_grad = along(keys_ref[s, :, 0:128], dscores) + along(later_ref[:, 0:128], dscores_ref[s])
        for i in range(2):
            low, high = slice(LEAF * i, LEAF * i + LEAF), slice(256 + LEAF * i, 256 + LEAF * i + LEAF)
            for cols, pair, scale in ((slice(0, 128), attended, 1.0), (slice(128, 256), query_grad, SCALE)):
                mine = jnp.concatenate([pair[:HEAD_DIM, low], pair[HEAD_DIM:, high]], axis=0).T
                results_refs[2 * s + i][:, cols] = (mine * scale).astype(BF16)
    block_ref[...] = totals[0] + totals[1]


def add(*parts):
    return functools.reduce(jnp.add, [p.astype(F32) for p in parts])


def scatter_kernel(
    block_ref, back2_ref, back4_ref, back6_ref, one_ref, zero_ref,
    slots_ref, own_ref, out1_ref, out2_ref, out3_ref, rows_ref,
):
    outer = lax.axis_index("outer")
    total = add(block_ref[...], back2_ref[0:128, :], back4_ref[0:128, :], back6_ref[0:128, :]).astype(BF16)
    for m in range(TEAM):
        slots_ref[outer * TEAM + m] = jnp.zeros((16, COLS), BF16)
        for c in range(4):
            rows = total[32 * c + 8 * m : 32 * c + 8 * m + 8]
            block = jnp.concatenate([rows[:, :COLS], rows[:, COLS:]], axis=0)
            for k in range(1 << c, 2 << c):
                slots_ref[(outer ^ k) * TEAM + m] = block
    total = add(back4_ref[128:192, :], back6_ref[128:192, :])
    count = 64
    for level in (back2_ref[128:256, :], one_ref[...], zero_ref[...]):
        write_rows(rows_ref, total, 0, 2)
        write_rows(rows_ref, total, 1, 2)
        count *= 2
        total = level.astype(F32) + HALF_ROOT * read_rows(rows_ref, count)
    own_ref[...] = total[0:LEAF]
    for k, ref in enumerate((out1_ref, out2_ref, out3_ref)):
        ref[...] = total[LEAF * (k + 1) : LEAF * (k + 2)].astype(BF16)


def outputs_kernel(own_ref, got1_ref, got2_ref, got3_ref, att_ref, dq_ref):
    for k, ref in enumerate((own_ref, got1_ref, got2_ref, got3_ref)):
        cols = columns(0, member() ^ k)
        att_ref[:, cols] = ref[:, :COLS]
        dq_ref[:, cols] = ref[:, COLS:]


def finish_kernel(slots_ref, own_ref, got1_ref, got2_ref, got3_ref, out_ref, sum_ref):
    outer = lax.axis_index("outer")
    row = row_index()
    four, five, six, seven = [
        jnp.concatenate([b[:8] for b in blocks] + [b[8:] for b in blocks], axis=1) for blocks in class_sums(slots_ref)
    ]
    five = spread(jnp.where(row & 1 == outer & 1, five, 0.0), 1)
    six = spread(spread(jnp.where(row & 3 == outer & 3, six, 0.0), 1), 2)
    seven = jnp.sum(jnp.where(row == outer & 7, seven, 0.0), axis=0, keepdims=True)
    total = four + HALF_ROOT * (five + HALF_ROOT * (six + HALF_ROOT * seven))
    total = total * 0.25
    for k, ref in enumerate((own_ref, got1_ref, got2_ref, got3_ref)):
        for start, cols in ((0, slice(0, COLS)), (D, slice(COLS, 2 * COLS))):
            sum_ref[:, columns(start, member() ^ k)] = ref[:, cols].astype(F32)
    for r in range(8):
        rows = slice(16 * r, 16 * r + 16)
        out_ref[rows, :] = (sum_ref[rows, :] + total[r : r + 1]).astype(BF16)


def shards(queries, keys_values, cotangent):
    queries, keys_values, cotangent = queries[0], keys_values[0], cotangent[0]
    slots = ((16 * TEAM, 16, COLS), BF16)
    whole = ((LEAF, D), BF16)
    piece = ((LEAF, 2 * COLS), BF16)
    own_rows = pltpu.VMEM((8, LEAF, 128), F32)
    team_rows = pltpu.VMEM((2, TEAM * LEAF, 128), F32)

    sent, own, out1, out2, out3 = call(pool_kernel, "pool", [slots, *[piece] * 4], [own_rows])(keys_values)
    taken = trade_slots(sent)
    got2, got3, got1 = exchange(out2, 2), exchange(out3, 3), exchange(out1, 1)
    own_q, out1, out2, out3 = call(pack_kernel, "pack", [piece] * 4)(queries, cotangent)
    tokens, one, near, far = call(
        collect_kernel, "collect", [((512, 256), BF16), ((256, 256), BF16), ((256, 256), BF16), ((192, 256), BF16)], [team_rows]
    )(taken, own, got1, got2, got3, own_q)
    got4 = exchange(far, 8)
    got6 = exchange(far, 12)
    near = exchange(near, 4)
    got2, got3, got1 = exchange(out2, 2), exchange(out3, 3), exchange(out1, 1)

    stacks = ((2, 512, 128), BF16)
    stat = ((2, 1, 512), F32)
    squares = ((2, 512, 512), F32)
    keys, q2, cot2, exps, dweights, top, sums, dots = call(
        first_kernel,
        "first",
        [((2, 512, 256), BF16), stacks, stacks, squares, squares, stat, stat, stat],
        flops=4 * 512 * 1024 * 128,
    )(own_q, got1, got2, got3, tokens, one, far)
    later = ((2, 640, 512), BF16)
    send2, send4, send6, later_keys, factor, centre, rounded, dscores = call(
        second_kernel,
        "second",
        [((256, 256), BF16), ((192, 256), BF16), ((192, 256), BF16), ((640, 256), BF16), stat, stat, later, later],
        flops=8 * 640 * 1024 * 128,
    )(near, got4, got6, q2, cot2, top, sums, dots)
    back4 = exchange(send4, 8)
    back6 = exchange(send6, 12)
    back2 = exchange(send2, 4)
    block, one, zero, own_results, out1, out2, out3 = call(
        rest_kernel,
        "rest",
        [((128, 256), F32), ((256, 256), F32), ((512, 256), F32), *[piece] * 4],
        flops=8 * 1152 * 1024 * 128,
    )(keys, later_keys, q2, cot2, exps, dweights, factor, centre, rounded, dscores)
    got2, got3, got1 = exchange(out2, 2), exchange(out3, 3), exchange(out1, 1)
    attended, query_grad = call(outputs_kernel, "outputs", [whole, whole])(own_results, got1, got2, got3)

    sent, own, out1, out2, out3 = call(
        scatter_kernel, "scatter", [slots, ((LEAF, 256), F32), *[piece] * 3], [team_rows]
    )(block, back2, back4, back6, one, zero)
    taken = trade_slots(sent)
    got2, got3, got1 = exchange(out2, 2), exchange(out3, 3), exchange(out1, 1)
    (kv_grad,) = call(finish_kernel, "finish", [((LEAF, 2 * D), BF16)], [pltpu.VMEM((LEAF, 2 * D), F32)])(
        taken, own, got1, got2, got3
    )
    return attended[None], query_grad[None], kv_grad[None]


def solution(mesh):
    spec = P(None, ("outer", "inner"), None)
    return jax.shard_map(shards, mesh=mesh, in_specs=(spec,) * 3, out_specs=(spec,) * 3, check_vma=False)
```

```python
import functools
import math

import jax
import jax.numpy as jnp
from jax import lax
from jax.experimental import pallas as pl
from jax.experimental.pallas import tpu as pltpu
from jax.sharding import PartitionSpec as P

LEAF = 128
D = 512
TEAM = 4
COLS = 128
HEAD_DIM = 64
LONG = 2 * 10**10
HALF_ROOT = 1.0 / math.sqrt(2.0)
SCALE = 1.0 / math.sqrt(HEAD_DIM)
BF16 = jnp.bfloat16
F32 = jnp.float32
VMEM = pl.BlockSpec(memory_space=pltpu.VMEM)
HBM = pl.BlockSpec(memory_space=pltpu.HBM)
ANYWHERE = pl.BlockSpec(memory_space=pl.ANY)


def call(body, name, outs, scratch=(), flops=0, spec=VMEM, limit=24, after=()):
    def run(*operands):
        count = len(operands)
        operands = (*operands, *after)
        shapes = [jax.ShapeDtypeStruct(shape, dtype) for shape, dtype in outs]
        moved = sum(math.prod(s.shape) * s.dtype.itemsize for s in (*operands, *shapes))
        return pl.pallas_call(
            (lambda *refs: body(*refs[:count], *refs[count + len(after) :])),
            out_shape=shapes,
            in_specs=[spec] * count + [ANYWHERE] * len(after),
            out_specs=[VMEM] * len(shapes),
            scratch_shapes=list(scratch),
            name=name,
            cost_estimate=pl.CostEstimate(flops=flops, bytes_accessed=moved, transcendentals=0),
            compiler_params=pltpu.CompilerParams(vmem_limit_bytes=limit * 1024 * 1024),
        )(*operands)

    return run


def exchange(array, bits):
    return lax.ppermute(array, "inner", [(i, i ^ bits) for i in range(16)])


def trade_slots(slots):
    groups = [[16 * o + 4 * team + m for o in range(16) for m in range(TEAM)] for team in range(4)]
    return lax.all_to_all(slots, ("outer", "inner"), 0, 0, axis_index_groups=groups, tiled=True)


def member():
    return lax.axis_index("inner") & 3


def columns(start, group):
    return pl.ds(pl.multiple_of(start + COLS * group, COLS), COLS)


def class_of(k):
    return k.bit_length() - 1


def row_index():
    return lax.broadcasted_iota(jnp.int32, (8, 2 * D), 0)


def read_rows(ref, count, first=0, step=1):
    return jnp.concatenate([ref[c, pl.ds(first, count, stride=step), :] for c in range(ref.shape[0])], axis=1)


def write_rows(ref, rows, first=0, step=1):
    for c in range(ref.shape[0]):
        ref[c, pl.ds(first, rows.shape[0], stride=step), :] = rows[:, 128 * c : 128 * c + 128]


def pool_rows(ref, count):
    pooled = ((read_rows(ref, count // 2, 0, 2) + read_rows(ref, count // 2, 1, 2)) * HALF_ROOT).astype(BF16)
    write_rows(ref, pooled.astype(F32))
    return pooled


def halve(rows, apart):
    pooled = (rows + pltpu.roll(rows, 8 - apart, 0)) * HALF_ROOT
    return pooled.astype(BF16).astype(F32)


def spread(rows, apart):
    row = row_index()
    return rows + jnp.where(row & apart == 0, pltpu.roll(rows, 8 - apart, 0), pltpu.roll(rows, apart, 0))


def pool_kernel(
    q_hbm, kv_hbm, cot_hbm, slots_ref, own_ref, out1_ref, out2_ref, out3_ref, q_ref, kv_ref, cot_ref, rows_ref, sems
):
    pairs = ((kv_hbm, kv_ref), (q_hbm, q_ref), (cot_hbm, cot_ref))
    copies = [pltpu.make_async_copy(a, b, sems.at[i]) for i, (a, b) in enumerate(pairs)]
    for copy in copies:
        copy.start()
    copies[0].wait()
    write_rows(rows_ref, kv_ref[...].astype(F32))
    for count in (128, 64, 32, 16):
        four = pool_rows(rows_ref, count)
    four = four.astype(F32)
    outer = lax.axis_index("outer")
    row = row_index()
    five = halve(four, 1)
    six = halve(five, 2)
    seven = halve(six, 4)
    five = jnp.where(row & 1 == 0, five, pltpu.roll(five, 1, 0))
    six = spread(spread(jnp.where(row & 3 == 0, six, 0.0), 1), 2)
    seven = jnp.broadcast_to(seven[:1], seven.shape)
    table = [
        four,
        jnp.where(row & 1 == outer & 1, five, 0.0),
        jnp.where(row & 3 == outer & 3, six, 0.0),
        jnp.where(row == outer & 7, seven, 0.0),
    ]
    for m in range(TEAM):
        keys, values = slice(COLS * m, COLS * m + COLS), slice(D + COLS * m, D + COLS * m + COLS)
        blocks = [jnp.concatenate([rows[:, keys], rows[:, values]], axis=0).astype(BF16) for rows in table]
        slots_ref[outer * TEAM + m] = jnp.zeros_like(blocks[0])
        for k in range(1, 16):
            slots_ref[(outer ^ k) * TEAM + m] = blocks[class_of(k)]
    copies[1].wait()
    copies[2].wait()
    for k, ref in enumerate((own_ref, out1_ref, out2_ref, out3_ref)):
        group = member() ^ k
        ref[:, 0:128] = q_ref[:, columns(0, group)]
        ref[:, 128:256] = kv_ref[:, columns(0, group)]
        ref[:, 256:384] = kv_ref[:, columns(D, group)]
        ref[:, 384:512] = cot_ref[:, columns(0, group)]


def class_sums(slots_ref):
    outer = lax.axis_index("outer")

    def total(c, m):
        return functools.reduce(jnp.add, [slots_ref[(outer ^ k) * TEAM + m].astype(F32) for k in range(1 << c, 2 << c)])

    return [[total(c, m) for m in range(TEAM)] for c in range(4)]


def side_by_side(block):
    return jnp.concatenate([block[:8], block[8:]], axis=1)


def team_kernel(own_ref, got1_ref, got2_ref, got3_ref, tokens_ref, one_ref, two_ref, three_ref, rows_ref):
    for k, ref in enumerate((own_ref, got1_ref, got2_ref, got3_ref)):
        tokens_ref[LEAF * k : LEAF * k + LEAF, :] = ref[...]
    write_rows(rows_ref, tokens_ref[:, 128:384].astype(F32))
    one_ref[...] = pool_rows(rows_ref, 512)
    two_ref[...] = pool_rows(rows_ref, 256)
    three_ref[...] = pool_rows(rows_ref, 128)


def collect_kernel(slots_ref, block_ref):
    block_ref[...] = jnp.concatenate(
        [side_by_side(b) for blocks in class_sums(slots_ref) for b in blocks], axis=0
    ).astype(BF16)


def low_kernel(two_ref, six_ref, four_ref, out_ref):
    out_ref[0:128, :] = two_ref[...]
    out_ref[128:192, :] = four_ref[...]
    out_ref[192:256, :] = six_ref[...]


def across(a, b):
    return lax.dot_general(a, b, (((1,), (1,)), ((), ())), preferred_element_type=F32)


def along(a, b):
    return lax.dot_general(a, b, (((0,), (0,)), ((), ())), preferred_element_type=F32)


def two_heads(block):
    low_half = lax.broadcasted_iota(jnp.int32, block.shape, 1) < HEAD_DIM
    return jnp.concatenate([jnp.where(low_half, block, 0.0), jnp.where(low_half, 0.0, block)], axis=0).astype(BF16)


def first_kernel(
    tokens_ref, one_ref, block_ref, low_ref, keys_ref, q2_ref, cot2_ref, exps_ref, dweights_ref, max_ref, sum_ref, dot_ref
):
    for s in range(2):
        tokens = slice(256 * s, 256 * s + 256)
        keys_ref[s, 0:256, :] = tokens_ref[tokens, 128:384]
        keys_ref[s, 256:384, :] = one_ref[128 - 128 * s : 256 - 128 * s, :]
        keys_ref[s, 384:512, :] = block_ref[...]
        keys_ref[s, 512:768, :] = low_ref[...]
        queries = two_heads(tokens_ref[tokens, 0:128].astype(F32) * SCALE)
        grads = two_heads(tokens_ref[tokens, 384:512].astype(F32))
        q2_ref[s] = queries
        cot2_ref[s] = grads
        scores = across(keys_ref[s, :, 0:128], queries)
        top = jnp.max(scores, axis=0, keepdims=True)
        exps = jnp.exp(scores - top)
        dweights = across(keys_ref[s, :, 128:256], grads)
        exps_ref[s] = exps
        dweights_ref[s] = dweights
        max_ref[s] = top
        sum_ref[s] = jnp.sum(exps, axis=0, keepdims=True)
        dot_ref[s] = jnp.sum(exps * dweights, axis=0, keepdims=True)


def second_kernel(
    got2_ref, got6_ref, got4_ref, low_ref, q2_ref, cot2_ref, exps_ref, dweights_ref, max_ref, sum_ref, dot_ref,
    send2_ref, send4_ref, send6_ref, keys_ref, factor_ref, centre_ref, rounded_ref, dscores_ref,
):
    keys_ref[0:128, :] = got2_ref[...]
    keys_ref[128:256, :] = got4_ref[...]
    keys_ref[256:384, :] = got6_ref[...]
    keys_ref[384:640, :] = low_ref[...]
    dkeys, dvals = [], []
    for s in range(2):
        queries, grads = q2_ref[s], cot2_ref[s]
        scores = across(keys_ref[0:384, 0:128], queries)
        dweights = across(keys_ref[0:384, 128:256], grads)
        top = jnp.maximum(max_ref[s], jnp.max(scores, axis=0, keepdims=True))
        exps = jnp.exp(scores - top)
        before = jnp.exp(max_ref[s] - top)
        inverse = 1.0 / (sum_ref[s] * before + jnp.sum(exps, axis=0, keepdims=True))
        centre = (dot_ref[s] * before + jnp.sum(exps * dweights, axis=0, keepdims=True)) * inverse
        factor = before * inverse
        weights = jnp.concatenate([exps * inverse, exps_ref[s, 512:768, :] * factor], axis=0)
        dweights = jnp.concatenate([dweights, dweights_ref[s, 512:768, :]], axis=0)
        rounded = weights.astype(BF16)
        dscores = (weights * (dweights - centre)).astype(BF16)
        factor_ref[s] = factor
        centre_ref[s] = centre
        rounded_ref[s] = rounded
        dscores_ref[s] = dscores
        dkeys.append(jnp.dot(dscores, queries, preferred_element_type=F32))
        dvals.append(jnp.dot(rounded, grads, preferred_element_type=F32))
    for cols, parts in ((slice(0, 128), dkeys), (slice(128, 256), dvals)):
        total = (parts[0] + parts[1]).astype(BF16)
        send2_ref[0:128, cols] = total[0:128]
        send2_ref[128:256, cols] = total[384:512]
        send4_ref[0:128, cols] = total[128:256]
        send4_ref[128:192, cols] = total[512:576]
        send6_ref[0:128, cols] = total[256:384]
        send6_ref[128:192, cols] = total[576:640]


def rest_kernel(
    keys_ref, later_ref, q2_ref, cot2_ref, exps_ref, dweights_ref, factor_ref, centre_ref, rounded_ref, dscores_ref,
    block_ref, one_ref, zero_ref, results_ref,
):
    totals = []
    for s in range(2):
        weights = exps_ref[s, 0:512, :] * factor_ref[s]
        rounded = weights.astype(BF16)
        dscores = (weights * (dweights_ref[s, 0:512, :] - centre_ref[s])).astype(BF16)
        dkeys = jnp.dot(dscores, q2_ref[s], preferred_element_type=F32)
        dvals = jnp.dot(rounded, cot2_ref[s], preferred_element_type=F32)
        total = jnp.concatenate([dkeys, dvals], axis=1)
        zero_ref[256 * s : 256 * s + 256, :] = total[0:256]
        one_ref[128 - 128 * s : 256 - 128 * s, :] = total[256:384]
        totals.append(total[384:512])
        attended = along(keys_ref[s, 0:512, 128:256], rounded) + along(later_ref[:, 128:256], rounded_ref[s])
        query_grad = along(keys_ref[s, 0:512, 0:128], dscores) + along(later_ref[:, 0:128], dscores_ref[s])
        for i in range(2):
            rows = slice(256 * s + LEAF * i, 256 * s + LEAF * i + LEAF)
            low, high = slice(LEAF * i, LEAF * i + LEAF), slice(256 + LEAF * i, 256 + LEAF * i + LEAF)
            for cols, pair, scale in ((slice(0, 128), attended, 1.0), (slice(128, 256), query_grad, SCALE)):
                mine = jnp.concatenate([pair[:HEAD_DIM, low], pair[HEAD_DIM:, high]], axis=0).T
                results_ref[rows, cols] = (mine * scale).astype(BF16)
    block_ref[...] = totals[0] + totals[1]


def add(*parts):
    return functools.reduce(jnp.add, [p.astype(F32) for p in parts])


def scatter_kernel(
    block_ref, back2_ref, back4_ref, back6_ref, one_ref, zero_ref, results_ref,
    slots_ref, own_ref, out1_ref, out2_ref, out3_ref, rows_ref,
):
    outer = lax.axis_index("outer")
    total = add(block_ref[...], back2_ref[0:128, :], back4_ref[0:128, :], back6_ref[0:128, :]).astype(BF16)
    for m in range(TEAM):
        slots_ref[outer * TEAM + m] = jnp.zeros((16, COLS), BF16)
        for c in range(4):
            rows = total[32 * c + 8 * m : 32 * c + 8 * m + 8]
            block = jnp.concatenate([rows[:, :COLS], rows[:, COLS:]], axis=0)
            for k in range(1 << c, 2 << c):
                slots_ref[(outer ^ k) * TEAM + m] = block
    total = add(back4_ref[128:192, :], back6_ref[128:192, :])
    count = 64
    for level in (back2_ref[128:256, :], one_ref[...], zero_ref[...]):
        write_rows(rows_ref, total, 0, 2)
        write_rows(rows_ref, total, 1, 2)
        count *= 2
        total = level.astype(F32) + HALF_ROOT * read_rows(rows_ref, count)
    own_ref[...] = total[0:LEAF]
    for k, ref in enumerate((out1_ref, out2_ref, out3_ref)):
        rows = slice(LEAF * (k + 1), LEAF * (k + 2))
        ref[:, 0:256] = total[rows].astype(BF16)
        ref[:, 256:512] = results_ref[rows, :]


def merge_kernel(results_ref, own_ref, got1_ref, got2_ref, got3_ref, att_ref, dq_ref, sum_ref):
    for k, ref in enumerate((own_ref, got1_ref, got2_ref, got3_ref)):
        group = member() ^ k
        sum_ref[:, columns(0, group)] = ref[:, 0:128].astype(F32)
        sum_ref[:, columns(D, group)] = ref[:, 128:256].astype(F32)
        part = results_ref[0:LEAF, :] if k == 0 else ref[:, 256:512]
        att_ref[:, columns(0, group)] = part[:, :COLS]
        dq_ref[:, columns(0, group)] = part[:, COLS:]


def finish_kernel(slots_ref, sum_ref, out_ref):
    outer = lax.axis_index("outer")
    row = row_index()
    four, five, six, seven = [
        jnp.concatenate([b[:8] for b in blocks] + [b[8:] for b in blocks], axis=1) for blocks in class_sums(slots_ref)
    ]
    five = spread(jnp.where(row & 1 == outer & 1, five, 0.0), 1)
    six = spread(spread(jnp.where(row & 3 == outer & 3, six, 0.0), 1), 2)
    seven = jnp.sum(jnp.where(row == outer & 7, seven, 0.0), axis=0, keepdims=True)
    total = four + HALF_ROOT * (five + HALF_ROOT * (six + HALF_ROOT * seven))
    total = total * 0.25
    for r in range(8):
        rows = slice(16 * r, 16 * r + 16)
        out_ref[rows, :] = (sum_ref[rows, :] + total[r : r + 1]).astype(BF16)


def shards(queries, keys_values, cotangent):
    queries, keys_values, cotangent = queries[0], keys_values[0], cotangent[0]
    slots = ((16 * TEAM, 16, COLS), BF16)
    piece = ((LEAF, D), BF16)
    loaded = [pltpu.VMEM((LEAF, D), BF16), pltpu.VMEM((LEAF, 2 * D), BF16), pltpu.VMEM((LEAF, D), BF16)]
    own_rows = pltpu.VMEM((8, LEAF, 128), F32)
    team_rows = pltpu.VMEM((2, TEAM * LEAF, 128), F32)

    sent, own, out1, out2, out3 = call(
        pool_kernel, "pool", [slots, piece, piece, piece, piece], [*loaded, own_rows, pltpu.SemaphoreType.DMA((3,))], spec=HBM, limit=56
    )(queries, keys_values, cotangent)
    taken = trade_slots(sent)
    got2 = exchange(out2, 2)
    got3 = exchange(out3, 3)
    got1 = exchange(out1, 1)
    tokens, one, two, three = call(
        team_kernel,
        "team",
        [((512, D), BF16), ((256, 256), BF16), ((128, 256), BF16), ((64, 256), BF16)],
        [team_rows],
        flops=LONG,
    )(own, got1, got2, got3)
    low4 = exchange(three, 8)
    low6 = exchange(three, 12)
    low2 = exchange(two, 4)
    (block,) = call(collect_kernel, "collect", [((128, 256), BF16)], flops=LONG)(taken)
    got4 = exchange(block, 8)
    got6 = exchange(block, 12)
    got2 = exchange(block, 4)
    (low,) = call(low_kernel, "low", [((256, 256), BF16)], flops=LONG)(low2, low6, low4)

    stacks = ((2, 512, 128), BF16)
    stat = ((2, 1, 512), F32)
    squares = ((2, 768, 512), F32)
    keys, q2, cot2, exps, dweights, top, sums, dots = call(
        first_kernel,
        "first",
        [((2, 768, 256), BF16), stacks, stacks, squares, squares, stat, stat, stat],
        flops=4 * 768 * 1024 * 128,
    )(tokens, one, block, low)
    later = ((2, 640, 512), BF16)
    send2, send4, send6, later_keys, factor, centre, rounded, dscores = call(
        second_kernel,
        "second",
        [((256, 256), BF16), ((192, 256), BF16), ((192, 256), BF16), ((640, 256), BF16), stat, stat, later, later],
        flops=8 * 640 * 1024 * 128,
    )(got2, got6, got4, low, q2, cot2, exps, dweights, top, sums, dots)
    back4 = exchange(send4, 8)
    back6 = exchange(send6, 12)
    back2 = exchange(send2, 4)
    block, one, zero, results = call(
        rest_kernel,
        "rest",
        [((128, 256), F32), ((256, 256), F32), ((512, 256), F32), ((512, 256), BF16)],
        flops=8 * 1152 * 1024 * 128,
    )(keys, later_keys, q2, cot2, exps, dweights, factor, centre, rounded, dscores)

    sent, own, out1, out2, out3 = call(
        scatter_kernel, "scatter", [slots, ((LEAF, 256), F32), piece, piece, piece], [team_rows]
    )(block, back2, back4, back6, one, zero, results)
    taken = trade_slots(sent)
    got2 = exchange(out2, 2)
    got3 = exchange(out3, 3)
    got1 = exchange(out1, 1)
    attended, query_grad, total = call(
        merge_kernel, "merge", [((LEAF, D), BF16), ((LEAF, D), BF16), ((LEAF, 2 * D), F32)], flops=LONG
    )(results, own, got1, got2, got3)
    (kv_grad,) = call(finish_kernel, "finish", [((LEAF, 2 * D), BF16)])(taken, total)
    return attended[None], query_grad[None], kv_grad[None]


def solution(mesh):
    spec = P(None, ("outer", "inner"), None)
    return jax.shard_map(shards, mesh=mesh, in_specs=(spec,) * 3, out_specs=(spec,) * 3, check_vma=False)
```

```python
import functools
import math

import jax
import jax.numpy as jnp
from jax import lax
from jax.experimental import pallas as pl
from jax.experimental.pallas import tpu as pltpu
from jax.sharding import PartitionSpec as P

LEAF = 128
D = 512
TEAM = 4
COLS = 128
HEAD_DIM = 64
LONG = 2 * 10**10
HALF_ROOT = 1.0 / math.sqrt(2.0)
SCALE = 1.0 / math.sqrt(HEAD_DIM)
BF16 = jnp.bfloat16
F32 = jnp.float32
VMEM = pl.BlockSpec(memory_space=pltpu.VMEM)
HBM = pl.BlockSpec(memory_space=pltpu.HBM)
ANYWHERE = pl.BlockSpec(memory_space=pl.ANY)


def call(body, name, outs, scratch=(), flops=0, spec=VMEM, limit=24, after=()):
    def run(*operands):
        count = len(operands)
        operands = (*operands, *after)
        shapes = [jax.ShapeDtypeStruct(shape, dtype) for shape, dtype in outs]
        moved = sum(math.prod(s.shape) * s.dtype.itemsize for s in (*operands, *shapes))
        return pl.pallas_call(
            (lambda *refs: body(*refs[:count], *refs[count + len(after) :])),
            out_shape=shapes,
            in_specs=[spec] * count + [ANYWHERE] * len(after),
            out_specs=[VMEM] * len(shapes),
            scratch_shapes=list(scratch),
            name=name,
            cost_estimate=pl.CostEstimate(flops=flops, bytes_accessed=moved, transcendentals=0),
            compiler_params=pltpu.CompilerParams(vmem_limit_bytes=int(limit * 1024 * 1024)),
        )(*operands)

    return run


def exchange(array, bits):
    return lax.ppermute(array, "inner", [(i, i ^ bits) for i in range(16)])


def trade_slots(slots):
    groups = [[16 * o + 4 * team + m for o in range(16) for m in range(TEAM)] for team in range(4)]
    return lax.all_to_all(slots, ("outer", "inner"), 0, 0, axis_index_groups=groups, tiled=True)


def member():
    return lax.axis_index("inner") & 3


def columns(start, group):
    return pl.ds(pl.multiple_of(start + COLS * group, COLS), COLS)


def class_of(k):
    return k.bit_length() - 1


def row_index():
    return lax.broadcasted_iota(jnp.int32, (8, 2 * D), 0)


def read_rows(ref, count, first=0, step=1):
    return jnp.concatenate([ref[c, pl.ds(first, count, stride=step), :] for c in range(ref.shape[0])], axis=1)


def write_rows(ref, rows, first=0, step=1):
    for c in range(ref.shape[0]):
        ref[c, pl.ds(first, rows.shape[0], stride=step), :] = rows[:, 128 * c : 128 * c + 128]


def pool_rows(ref, count):
    pooled = ((read_rows(ref, count // 2, 0, 2) + read_rows(ref, count // 2, 1, 2)) * HALF_ROOT).astype(BF16)
    write_rows(ref, pooled.astype(F32))
    return pooled


def halve(rows, apart):
    pooled = (rows + pltpu.roll(rows, 8 - apart, 0)) * HALF_ROOT
    return pooled.astype(BF16).astype(F32)


def spread(rows, apart):
    row = row_index()
    return rows + jnp.where(row & apart == 0, pltpu.roll(rows, 8 - apart, 0), pltpu.roll(rows, apart, 0))


def pool_kernel(
    q_hbm, kv_hbm, cot_hbm, slots_ref, own_ref, out1_ref, out2_ref, out3_ref, q_ref, kv_ref, cot_ref, rows_ref, sems
):
    pairs = ((kv_hbm, kv_ref), (q_hbm, q_ref), (cot_hbm, cot_ref))
    copies = [pltpu.make_async_copy(a, b, sems.at[i]) for i, (a, b) in enumerate(pairs)]
    for copy in copies:
        copy.start()
    copies[0].wait()
    write_rows(rows_ref, kv_ref[...].astype(F32))
    for count in (128, 64, 32, 16):
        four = pool_rows(rows_ref, count)
    four = four.astype(F32)
    outer = lax.axis_index("outer")
    row = row_index()
    five = halve(four, 1)
    six = halve(five, 2)
    seven = halve(six, 4)
    five = jnp.where(row & 1 == 0, five, pltpu.roll(five, 1, 0))
    six = spread(spread(jnp.where(row & 3 == 0, six, 0.0), 1), 2)
    seven = jnp.broadcast_to(seven[:1], seven.shape)
    table = [
        four,
        jnp.where(row & 1 == outer & 1, five, 0.0),
        jnp.where(row & 3 == outer & 3, six, 0.0),
        jnp.where(row == outer & 7, seven, 0.0),
    ]
    for m in range(TEAM):
        keys, values = slice(COLS * m, COLS * m + COLS), slice(D + COLS * m, D + COLS * m + COLS)
        blocks = [jnp.concatenate([rows[:, keys], rows[:, values]], axis=0).astype(BF16) for rows in table]
        slots_ref[outer * TEAM + m] = jnp.zeros_like(blocks[0])
        for k in range(1, 16):
            slots_ref[(outer ^ k) * TEAM + m] = blocks[class_of(k)]
    copies[1].wait()
    copies[2].wait()
    for k, ref in enumerate((own_ref, out1_ref, out2_ref, out3_ref)):
        group = member() ^ k
        ref[:, 0:128] = q_ref[:, columns(0, group)]
        ref[:, 128:256] = kv_ref[:, columns(0, group)]
        ref[:, 256:384] = kv_ref[:, columns(D, group)]
        ref[:, 384:512] = cot_ref[:, columns(0, group)]


def class_sums(slots_ref):
    outer = lax.axis_index("outer")

    def total(c, m):
        return functools.reduce(jnp.add, [slots_ref[(outer ^ k) * TEAM + m].astype(F32) for k in range(1 << c, 2 << c)])

    return [[total(c, m) for m in range(TEAM)] for c in range(4)]


def side_by_side(block):
    return jnp.concatenate([block[:8], block[8:]], axis=1)


def team_kernel(own_ref, got1_ref, got2_ref, got3_ref, tokens_ref, one_ref, two_ref, three_ref, rows_ref):
    for k, ref in enumerate((own_ref, got1_ref, got2_ref, got3_ref)):
        tokens_ref[LEAF * k : LEAF * k + LEAF, :] = ref[...]
    write_rows(rows_ref, tokens_ref[:, 128:384].astype(F32))
    one_ref[...] = pool_rows(rows_ref, 512)
    two_ref[...] = pool_rows(rows_ref, 256)
    three_ref[...] = pool_rows(rows_ref, 128)


def collect_kernel(slots_ref, block_ref):
    block_ref[...] = jnp.concatenate(
        [side_by_side(b) for blocks in class_sums(slots_ref) for b in blocks], axis=0
    ).astype(BF16)


def low_kernel(two_ref, six_ref, four_ref, out_ref):
    out_ref[0:128, :] = two_ref[...]
    out_ref[128:192, :] = four_ref[...]
    out_ref[192:256, :] = six_ref[...]


def across(a, b):
    return lax.dot_general(a, b, (((1,), (1,)), ((), ())), preferred_element_type=F32)


def along(a, b):
    return lax.dot_general(a, b, (((0,), (0,)), ((), ())), preferred_element_type=F32)


def two_heads(block):
    low_half = lax.broadcasted_iota(jnp.int32, block.shape, 1) < HEAD_DIM
    return jnp.concatenate([jnp.where(low_half, block, 0.0), jnp.where(low_half, 0.0, block)], axis=0).astype(BF16)


def first_kernel(
    tokens_ref, one_ref, block_ref, low_ref, keys_ref, q2_ref, cot2_ref, exps_ref, dweights_ref, max_ref, sum_ref, dot_ref
):
    for s in range(2):
        tokens = slice(256 * s, 256 * s + 256)
        keys_ref[s, 0:256, :] = tokens_ref[tokens, 128:384]
        keys_ref[s, 256:384, :] = one_ref[128 - 128 * s : 256 - 128 * s, :]
        keys_ref[s, 384:512, :] = block_ref[...]
        keys_ref[s, 512:768, :] = low_ref[...]
        queries = two_heads(tokens_ref[tokens, 0:128].astype(F32) * SCALE)
        grads = two_heads(tokens_ref[tokens, 384:512].astype(F32))
        q2_ref[s] = queries
        cot2_ref[s] = grads
        scores = across(keys_ref[s, :, 0:128], queries)
        top = jnp.max(scores, axis=0, keepdims=True)
        exps = jnp.exp(scores - top)
        dweights = across(keys_ref[s, :, 128:256], grads)
        exps_ref[s] = exps
        dweights_ref[s] = dweights
        max_ref[s] = top
        sum_ref[s] = jnp.sum(exps, axis=0, keepdims=True)
        dot_ref[s] = jnp.sum(exps * dweights, axis=0, keepdims=True)


def second_kernel(
    got2_ref, got6_ref, got4_ref, low_ref, q2_ref, cot2_ref, exps_ref, dweights_ref, max_ref, sum_ref, dot_ref,
    send2_ref, send4_ref, send6_ref, keys_ref, factor_ref, centre_ref, rounded_ref, dscores_ref,
):
    keys_ref[0:128, :] = got2_ref[...]
    keys_ref[128:256, :] = got4_ref[...]
    keys_ref[256:384, :] = got6_ref[...]
    keys_ref[384:640, :] = low_ref[...]
    dkeys, dvals = [], []
    for s in range(2):
        queries, grads = q2_ref[s], cot2_ref[s]
        scores = across(keys_ref[0:384, 0:128], queries)
        dweights = across(keys_ref[0:384, 128:256], grads)
        top = jnp.maximum(max_ref[s], jnp.max(scores, axis=0, keepdims=True))
        exps = jnp.exp(scores - top)
        before = jnp.exp(max_ref[s] - top)
        inverse = 1.0 / (sum_ref[s] * before + jnp.sum(exps, axis=0, keepdims=True))
        centre = (dot_ref[s] * before + jnp.sum(exps * dweights, axis=0, keepdims=True)) * inverse
        factor = before * inverse
        weights = jnp.concatenate([exps * inverse, exps_ref[s, 512:768, :] * factor], axis=0)
        dweights = jnp.concatenate([dweights, dweights_ref[s, 512:768, :]], axis=0)
        rounded = weights.astype(BF16)
        dscores = (weights * (dweights - centre)).astype(BF16)
        factor_ref[s] = factor
        centre_ref[s] = centre
        rounded_ref[s] = rounded
        dscores_ref[s] = dscores
        dkeys.append(jnp.dot(dscores, queries, preferred_element_type=F32))
        dvals.append(jnp.dot(rounded, grads, preferred_element_type=F32))
    for cols, parts in ((slice(0, 128), dkeys), (slice(128, 256), dvals)):
        total = (parts[0] + parts[1]).astype(BF16)
        send2_ref[0:128, cols] = total[0:128]
        send2_ref[128:256, cols] = total[384:512]
        send4_ref[0:128, cols] = total[128:256]
        send4_ref[128:192, cols] = total[512:576]
        send6_ref[0:128, cols] = total[256:384]
        send6_ref[128:192, cols] = total[576:640]


def rest_kernel(
    keys_ref, later_ref, q2_ref, cot2_ref, exps_ref, dweights_ref, factor_ref, centre_ref, rounded_ref, dscores_ref,
    block_ref, one_ref, zero_ref, results_ref,
):
    totals = []
    for s in range(2):
        weights = exps_ref[s, 0:512, :] * factor_ref[s]
        rounded = weights.astype(BF16)
        dscores = (weights * (dweights_ref[s, 0:512, :] - centre_ref[s])).astype(BF16)
        dkeys = jnp.dot(dscores, q2_ref[s], preferred_element_type=F32)
        dvals = jnp.dot(rounded, cot2_ref[s], preferred_element_type=F32)
        total = jnp.concatenate([dkeys, dvals], axis=1)
        zero_ref[256 * s : 256 * s + 256, :] = total[0:256]
        one_ref[128 - 128 * s : 256 - 128 * s, :] = total[256:384]
        totals.append(total[384:512])
        attended = along(keys_ref[s, 0:512, 128:256], rounded) + along(later_ref[:, 128:256], rounded_ref[s])
        query_grad = along(keys_ref[s, 0:512, 0:128], dscores) + along(later_ref[:, 0:128], dscores_ref[s])
        for i in range(2):
            rows = slice(256 * s + LEAF * i, 256 * s + LEAF * i + LEAF)
            low, high = slice(LEAF * i, LEAF * i + LEAF), slice(256 + LEAF * i, 256 + LEAF * i + LEAF)
            for cols, pair, scale in ((slice(0, 128), attended, 1.0), (slice(128, 256), query_grad, SCALE)):
                mine = jnp.concatenate([pair[:HEAD_DIM, low], pair[HEAD_DIM:, high]], axis=0).T
                results_ref[rows, cols] = (mine * scale).astype(BF16)
    block_ref[...] = totals[0] + totals[1]


def add(*parts):
    return functools.reduce(jnp.add, [p.astype(F32) for p in parts])


def hold_kernel(got_ref, out_ref):
    out_ref[...] = got_ref[...]


def scatter_kernel(
    block_ref, back2_ref, back4_ref, back6_ref, one_ref, zero_ref, results_ref,
    slots_ref, own_ref, out1_ref, out2_ref, out3_ref, rows_ref,
):
    outer = lax.axis_index("outer")
    total = add(block_ref[...], back2_ref[0:128, :], back4_ref[0:128, :], back6_ref[0:128, :]).astype(BF16)
    for m in range(TEAM):
        slots_ref[outer * TEAM + m] = jnp.zeros((16, COLS), BF16)
        for c in range(4):
            rows = total[32 * c + 8 * m : 32 * c + 8 * m + 8]
            block = jnp.concatenate([rows[:, :COLS], rows[:, COLS:]], axis=0)
            for k in range(1 << c, 2 << c):
                slots_ref[(outer ^ k) * TEAM + m] = block
    total = add(back4_ref[128:192, :], back6_ref[128:192, :])
    count = 64
    for level in (back2_ref[128:256, :], one_ref[...], zero_ref[...]):
        write_rows(rows_ref, total, 0, 2)
        write_rows(rows_ref, total, 1, 2)
        count *= 2
        total = level.astype(F32) + HALF_ROOT * read_rows(rows_ref, count)
    own_ref[...] = total[0:LEAF]
    for k, ref in enumerate((out1_ref, out2_ref, out3_ref)):
        rows = slice(LEAF * (k + 1), LEAF * (k + 2))
        ref[:, 0:256] = total[rows].astype(BF16)
        ref[:, 256:512] = results_ref[rows, :]


def merge_kernel(results_ref, own_ref, got1_ref, got2_ref, got3_ref, att_ref, dq_ref, sum_ref):
    for k, ref in enumerate((own_ref, got1_ref, got2_ref, got3_ref)):
        group = member() ^ k
        sum_ref[:, columns(0, group)] = ref[:, 0:128].astype(F32)
        sum_ref[:, columns(D, group)] = ref[:, 128:256].astype(F32)
        part = results_ref[0:LEAF, :] if k == 0 else ref[:, 256:512]
        att_ref[:, columns(0, group)] = part[:, :COLS]
        dq_ref[:, columns(0, group)] = part[:, COLS:]


def finish_kernel(slots_ref, sum_ref, out_ref):
    outer = lax.axis_index("outer")
    row = row_index()
    four, five, six, seven = [
        jnp.concatenate([b[:8] for b in blocks] + [b[8:] for b in blocks], axis=1) for blocks in class_sums(slots_ref)
    ]
    five = spread(jnp.where(row & 1 == outer & 1, five, 0.0), 1)
    six = spread(spread(jnp.where(row & 3 == outer & 3, six, 0.0), 1), 2)
    seven = jnp.sum(jnp.where(row == outer & 7, seven, 0.0), axis=0, keepdims=True)
    total = four + HALF_ROOT * (five + HALF_ROOT * (six + HALF_ROOT * seven))
    total = total * 0.25
    for r in range(8):
        rows = slice(16 * r, 16 * r + 16)
        out_ref[rows, :] = (sum_ref[rows, :] + total[r : r + 1]).astype(BF16)


def shards(queries, keys_values, cotangent):
    queries, keys_values, cotangent = queries[0], keys_values[0], cotangent[0]
    slots = ((16 * TEAM, 16, COLS), BF16)
    piece = ((LEAF, D), BF16)
    loaded = [pltpu.VMEM((LEAF, D), BF16), pltpu.VMEM((LEAF, 2 * D), BF16), pltpu.VMEM((LEAF, D), BF16)]
    own_rows = pltpu.VMEM((8, LEAF, 128), F32)
    team_rows = pltpu.VMEM((2, TEAM * LEAF, 128), F32)

    sent, own, out1, out2, out3 = call(
        pool_kernel, "pool", [slots, piece, piece, piece, piece], [*loaded, own_rows, pltpu.SemaphoreType.DMA((3,))], spec=HBM, limit=53.375
    )(queries, keys_values, cotangent)
    taken = trade_slots(sent)
    got2 = exchange(out2, 2)
    got3 = exchange(out3, 3)
    got1 = exchange(out1, 1)
    tokens, one, two, three = call(
        team_kernel,
        "team",
        [((512, D), BF16), ((256, 256), BF16), ((128, 256), BF16), ((64, 256), BF16)],
        [team_rows],
        flops=LONG,
    )(own, got1, got2, got3)
    low4 = exchange(three, 8)
    low6 = exchange(three, 12)
    low2 = exchange(two, 4)
    (block,) = call(collect_kernel, "collect", [((128, 256), BF16)], flops=LONG)(taken)
    got4 = exchange(block, 8)
    got6 = exchange(block, 12)
    got2 = exchange(block, 4)
    (low,) = call(low_kernel, "low", [((256, 256), BF16)], flops=LONG)(low2, low6, low4)

    stacks = ((2, 512, 128), BF16)
    stat = ((2, 1, 512), F32)
    squares = ((2, 768, 512), F32)
    keys, q2, cot2, exps, dweights, top, sums, dots = call(
        first_kernel,
        "first",
        [((2, 768, 256), BF16), stacks, stacks, squares, squares, stat, stat, stat],
        flops=4 * 768 * 1024 * 128,
    )(tokens, one, block, low)
    later = ((2, 640, 512), BF16)
    send2, send4, send6, later_keys, factor, centre, rounded, dscores = call(
        second_kernel,
        "second",
        [((256, 256), BF16), ((192, 256), BF16), ((192, 256), BF16), ((640, 256), BF16), stat, stat, later, later],
        flops=8 * 640 * 1024 * 128,
    )(got2, got6, got4, low, q2, cot2, exps, dweights, top, sums, dots)
    back4 = exchange(send4, 8)
    back6 = exchange(send6, 12)
    back2 = exchange(send2, 4)
    block, one, zero, results = call(
        rest_kernel,
        "rest",
        [((128, 256), F32), ((256, 256), F32), ((512, 256), F32), ((512, 256), BF16)],
        flops=8 * 1152 * 1024 * 128,
    )(keys, later_keys, q2, cot2, exps, dweights, factor, centre, rounded, dscores)

    (back4,) = call(hold_kernel, "hold", [((192, 256), BF16)], flops=LONG)(back4)
    sent, own, out1, out2, out3 = call(
        scatter_kernel, "scatter", [slots, ((LEAF, 256), F32), piece, piece, piece], [team_rows]
    )(block, back2, back4, back6, one, zero, results)
    taken = trade_slots(sent)
    got2 = exchange(out2, 2)
    got3 = exchange(out3, 3)
    got1 = exchange(out1, 1)
    attended, query_grad, total = call(
        merge_kernel, "merge", [((LEAF, D), BF16), ((LEAF, D), BF16), ((LEAF, 2 * D), F32)], flops=LONG
    )(results, own, got1, got2, got3)
    (kv_grad,) = call(finish_kernel, "finish", [((LEAF, 2 * D), BF16)])(taken, total)
    return attended[None], query_grad[None], kv_grad[None]


def solution(mesh):
    spec = P(None, ("outer", "inner"), None)
    return jax.shard_map(shards, mesh=mesh, in_specs=(spec,) * 3, out_specs=(spec,) * 3, check_vma=False)
```

```python
import functools
import math

import jax
import jax.numpy as jnp
from jax import lax
from jax.experimental import pallas as pl
from jax.experimental.pallas import tpu as pltpu
from jax.sharding import PartitionSpec as P

LEAF = 128
D = 512
TEAM = 4
COLS = 128
HEAD_DIM = 64
LONG = 2 * 10**10
HALF_ROOT = 1.0 / math.sqrt(2.0)
SCALE = 1.0 / math.sqrt(HEAD_DIM)
BF16 = jnp.bfloat16
F32 = jnp.float32
VMEM = pl.BlockSpec(memory_space=pltpu.VMEM)
HBM = pl.BlockSpec(memory_space=pltpu.HBM)
ANYWHERE = pl.BlockSpec(memory_space=pl.ANY)


def call(body, name, outs, scratch=(), flops=0, spec=VMEM, limit=24, after=(), sent_first=False):
    def run(*operands):
        count = len(operands)
        operands = (*operands, *after)
        shapes = [jax.ShapeDtypeStruct(shape, dtype) for shape, dtype in outs]
        moved = sum(math.prod(s.shape) * s.dtype.itemsize for s in (*operands, *shapes))
        return pl.pallas_call(
            (lambda *refs: body(*refs[:count], *refs[count + len(after) :])),
            out_shape=shapes,
            in_specs=[spec] * count + [ANYWHERE] * len(after),
            out_specs=[HBM if sent_first and i == 0 else VMEM for i in range(len(shapes))],
            scratch_shapes=list(scratch),
            name=name,
            cost_estimate=pl.CostEstimate(flops=flops, bytes_accessed=moved, transcendentals=0),
            compiler_params=pltpu.CompilerParams(vmem_limit_bytes=int(limit * 1024 * 1024)),
        )(*operands)

    return run


def exchange(array, bits):
    return lax.ppermute(array, "inner", [(i, i ^ bits) for i in range(16)])


def trade_slots(slots):
    groups = [[16 * o + 4 * team + m for o in range(16) for m in range(TEAM)] for team in range(4)]
    return lax.all_to_all(slots, ("outer", "inner"), 0, 0, axis_index_groups=groups, tiled=True)


def member():
    return lax.axis_index("inner") & 3


def columns(start, group):
    return pl.ds(pl.multiple_of(start + COLS * group, COLS), COLS)


def class_of(k):
    return k.bit_length() - 1


def row_index():
    return lax.broadcasted_iota(jnp.int32, (8, 2 * D), 0)


def read_rows(ref, count, first=0, step=1):
    return jnp.concatenate([ref[c, pl.ds(first, count, stride=step), :] for c in range(ref.shape[0])], axis=1)


def write_rows(ref, rows, first=0, step=1):
    for c in range(ref.shape[0]):
        ref[c, pl.ds(first, rows.shape[0], stride=step), :] = rows[:, 128 * c : 128 * c + 128]


def pool_rows(ref, count):
    pooled = ((read_rows(ref, count // 2, 0, 2) + read_rows(ref, count // 2, 1, 2)) * HALF_ROOT).astype(BF16)
    write_rows(ref, pooled.astype(F32))
    return pooled


def halve(rows, apart):
    pooled = (rows + pltpu.roll(rows, 8 - apart, 0)) * HALF_ROOT
    return pooled.astype(BF16).astype(F32)


def spread(rows, apart):
    row = row_index()
    return rows + jnp.where(row & apart == 0, pltpu.roll(rows, 8 - apart, 0), pltpu.roll(rows, apart, 0))


def pool_kernel(
    q_hbm, kv_hbm, cot_hbm, slots_hbm, own_ref, out1_ref, out2_ref, out3_ref, q_ref, kv_ref, cot_ref, rows_ref, slots_ref, sems
):
    pairs = ((kv_hbm, kv_ref), (q_hbm, q_ref), (cot_hbm, cot_ref))
    copies = [pltpu.make_async_copy(a, b, sems.at[i]) for i, (a, b) in enumerate(pairs)]
    for copy in copies:
        copy.start()
    copies[0].wait()
    write_rows(rows_ref, kv_ref[...].astype(F32))
    for count in (128, 64, 32, 16):
        four = pool_rows(rows_ref, count)
    four = four.astype(F32)
    outer = lax.axis_index("outer")
    row = row_index()
    five = halve(four, 1)
    six = halve(five, 2)
    seven = halve(six, 4)
    five = jnp.where(row & 1 == 0, five, pltpu.roll(five, 1, 0))
    six = spread(spread(jnp.where(row & 3 == 0, six, 0.0), 1), 2)
    seven = jnp.broadcast_to(seven[:1], seven.shape)
    table = [
        four,
        jnp.where(row & 1 == outer & 1, five, 0.0),
        jnp.where(row & 3 == outer & 3, six, 0.0),
        jnp.where(row == outer & 7, seven, 0.0),
    ]
    for m in range(TEAM):
        keys, values = slice(COLS * m, COLS * m + COLS), slice(D + COLS * m, D + COLS * m + COLS)
        blocks = [jnp.concatenate([rows[:, keys], rows[:, values]], axis=0).astype(BF16) for rows in table]
        slots_ref[outer * TEAM + m] = jnp.zeros_like(blocks[0])
        for k in range(1, 16):
            slots_ref[(outer ^ k) * TEAM + m] = blocks[class_of(k)]
    sent = pltpu.make_async_copy(slots_ref, slots_hbm, sems.at[3])
    sent.start()
    copies[1].wait()
    copies[2].wait()
    for k, ref in enumerate((own_ref, out1_ref, out2_ref, out3_ref)):
        group = member() ^ k
        ref[:, 0:128] = q_ref[:, columns(0, group)]
        ref[:, 128:256] = kv_ref[:, columns(0, group)]
        ref[:, 256:384] = kv_ref[:, columns(D, group)]
        ref[:, 384:512] = cot_ref[:, columns(0, group)]
    sent.wait()


def class_sums(slots_ref):
    outer = lax.axis_index("outer")

    def total(c, m):
        return functools.reduce(jnp.add, [slots_ref[(outer ^ k) * TEAM + m].astype(F32) for k in range(1 << c, 2 << c)])

    return [[total(c, m) for m in range(TEAM)] for c in range(4)]


def side_by_side(block):
    return jnp.concatenate([block[:8], block[8:]], axis=1)


def team_kernel(own_ref, got1_ref, got2_ref, got3_ref, tokens_ref, one_ref, two_ref, three_ref, rows_ref):
    for k, ref in enumerate((own_ref, got1_ref, got2_ref, got3_ref)):
        tokens_ref[LEAF * k : LEAF * k + LEAF, :] = ref[...]
    write_rows(rows_ref, tokens_ref[:, 128:384].astype(F32))
    one_ref[...] = pool_rows(rows_ref, 512)
    two_ref[...] = pool_rows(rows_ref, 256)
    three_ref[...] = pool_rows(rows_ref, 128)


def collect_kernel(slots_ref, block_ref):
    block_ref[...] = jnp.concatenate(
        [side_by_side(b) for blocks in class_sums(slots_ref) for b in blocks], axis=0
    ).astype(BF16)


def low_kernel(two_ref, six_ref, four_ref, out_ref):
    out_ref[0:128, :] = two_ref[...]
    out_ref[128:192, :] = four_ref[...]
    out_ref[192:256, :] = six_ref[...]


def across(a, b):
    return lax.dot_general(a, b, (((1,), (1,)), ((), ())), preferred_element_type=F32)


def along(a, b):
    return lax.dot_general(a, b, (((0,), (0,)), ((), ())), preferred_element_type=F32)


def two_heads(block):
    low_half = lax.broadcasted_iota(jnp.int32, block.shape, 1) < HEAD_DIM
    return jnp.concatenate([jnp.where(low_half, block, 0.0), jnp.where(low_half, 0.0, block)], axis=0).astype(BF16)


def first_kernel(
    tokens_ref, one_ref, block_ref, low_ref, keys_ref, q2_ref, cot2_ref, exps_ref, dweights_ref, max_ref, sum_ref, dot_ref
):
    for s in range(2):
        tokens = slice(256 * s, 256 * s + 256)
        keys_ref[s, 0:256, :] = tokens_ref[tokens, 128:384]
        keys_ref[s, 256:384, :] = one_ref[128 - 128 * s : 256 - 128 * s, :]
        keys_ref[s, 384:512, :] = block_ref[...]
        keys_ref[s, 512:768, :] = low_ref[...]
        queries = two_heads(tokens_ref[tokens, 0:128].astype(F32) * SCALE)
        grads = two_heads(tokens_ref[tokens, 384:512].astype(F32))
        q2_ref[s] = queries
        cot2_ref[s] = grads
        scores = across(keys_ref[s, :, 0:128], queries)
        top = jnp.max(scores, axis=0, keepdims=True)
        exps = jnp.exp(scores - top)
        dweights = across(keys_ref[s, :, 128:256], grads)
        exps_ref[s] = exps
        dweights_ref[s] = dweights
        max_ref[s] = top
        sum_ref[s] = jnp.sum(exps, axis=0, keepdims=True)
        dot_ref[s] = jnp.sum(exps * dweights, axis=0, keepdims=True)


def second_kernel(
    got2_ref, got6_ref, got4_ref, low_ref, q2_ref, cot2_ref, exps_ref, dweights_ref, max_ref, sum_ref, dot_ref,
    send2_ref, send4_ref, send6_ref, keys_ref, factor_ref, centre_ref, rounded_ref, dscores_ref,
):
    keys_ref[0:128, :] = got2_ref[...]
    keys_ref[128:256, :] = got4_ref[...]
    keys_ref[256:384, :] = got6_ref[...]
    keys_ref[384:640, :] = low_ref[...]
    dkeys, dvals = [], []
    for s in range(2):
        queries, grads = q2_ref[s], cot2_ref[s]
        scores = across(keys_ref[0:384, 0:128], queries)
        dweights = across(keys_ref[0:384, 128:256], grads)
        top = jnp.maximum(max_ref[s], jnp.max(scores, axis=0, keepdims=True))
        exps = jnp.exp(scores - top)
        before = jnp.exp(max_ref[s] - top)
        inverse = 1.0 / (sum_ref[s] * before + jnp.sum(exps, axis=0, keepdims=True))
        centre = (dot_ref[s] * before + jnp.sum(exps * dweights, axis=0, keepdims=True)) * inverse
        factor = before * inverse
        weights = jnp.concatenate([exps * inverse, exps_ref[s, 512:768, :] * factor], axis=0)
        dweights = jnp.concatenate([dweights, dweights_ref[s, 512:768, :]], axis=0)
        rounded = weights.astype(BF16)
        dscores = (weights * (dweights - centre)).astype(BF16)
        factor_ref[s] = factor
        centre_ref[s] = centre
        rounded_ref[s] = rounded
        dscores_ref[s] = dscores
        dkeys.append(jnp.dot(dscores, queries, preferred_element_type=F32))
        dvals.append(jnp.dot(rounded, grads, preferred_element_type=F32))
    for cols, parts in ((slice(0, 128), dkeys), (slice(128, 256), dvals)):
        total = (parts[0] + parts[1]).astype(BF16)
        send2_ref[0:128, cols] = total[0:128]
        send2_ref[128:256, cols] = total[384:512]
        send4_ref[0:128, cols] = total[128:256]
        send4_ref[128:192, cols] = total[512:576]
        send6_ref[0:128, cols] = total[256:384]
        send6_ref[128:192, cols] = total[576:640]


def rest_kernel(
    keys_ref, later_ref, q2_ref, cot2_ref, exps_ref, dweights_ref, factor_ref, centre_ref, rounded_ref, dscores_ref,
    block_ref, one_ref, zero_ref, results_ref,
):
    totals = []
    for s in range(2):
        weights = exps_ref[s, 0:512, :] * factor_ref[s]
        rounded = weights.astype(BF16)
        dscores = (weights * (dweights_ref[s, 0:512, :] - centre_ref[s])).astype(BF16)
        dkeys = jnp.dot(dscores, q2_ref[s], preferred_element_type=F32)
        dvals = jnp.dot(rounded, cot2_ref[s], preferred_element_type=F32)
        total = jnp.concatenate([dkeys, dvals], axis=1)
        zero_ref[256 * s : 256 * s + 256, :] = total[0:256]
        one_ref[128 - 128 * s : 256 - 128 * s, :] = total[256:384]
        totals.append(total[384:512])
        attended = along(keys_ref[s, 0:512, 128:256], rounded) + along(later_ref[:, 128:256], rounded_ref[s])
        query_grad = along(keys_ref[s, 0:512, 0:128], dscores) + along(later_ref[:, 0:128], dscores_ref[s])
        for i in range(2):
            rows = slice(256 * s + LEAF * i, 256 * s + LEAF * i + LEAF)
            low, high = slice(LEAF * i, LEAF * i + LEAF), slice(256 + LEAF * i, 256 + LEAF * i + LEAF)
            for cols, pair, scale in ((slice(0, 128), attended, 1.0), (slice(128, 256), query_grad, SCALE)):
                mine = jnp.concatenate([pair[:HEAD_DIM, low], pair[HEAD_DIM:, high]], axis=0).T
                results_ref[rows, cols] = (mine * scale).astype(BF16)
    block_ref[...] = totals[0] + totals[1]


def add(*parts):
    return functools.reduce(jnp.add, [p.astype(F32) for p in parts])


def hold_kernel(got_ref, out_ref):
    out_ref[...] = got_ref[...]


def scatter_kernel(
    block_ref, back2_ref, back4_ref, back6_ref, one_ref, zero_ref, results_ref,
    slots_hbm, own_ref, near_ref, far_ref, rows_ref, slots_ref, sem,
):
    outer = lax.axis_index("outer")
    total = add(block_ref[...], back2_ref[0:128, :], back4_ref[0:128, :], back6_ref[0:128, :]).astype(BF16)
    for m in range(TEAM):
        slots_ref[outer * TEAM + m] = jnp.zeros((16, COLS), BF16)
        for c in range(4):
            rows = total[32 * c + 8 * m : 32 * c + 8 * m + 8]
            block = jnp.concatenate([rows[:, :COLS], rows[:, COLS:]], axis=0)
            for k in range(1 << c, 2 << c):
                slots_ref[(outer ^ k) * TEAM + m] = block
    sent = pltpu.make_async_copy(slots_ref, slots_hbm, sem)
    sent.start()
    total = add(back4_ref[128:192, :], back6_ref[128:192, :])
    count = 64
    for level in (back2_ref[128:256, :], one_ref[...], zero_ref[...]):
        write_rows(rows_ref, total, 0, 2)
        write_rows(rows_ref, total, 1, 2)
        count *= 2
        total = level.astype(F32) + HALF_ROOT * read_rows(rows_ref, count)
    own_ref[...] = total[0:LEAF]
    for k, ref in enumerate((near_ref, far_ref.at[0:LEAF, :], far_ref.at[LEAF : 2 * LEAF, :])):
        rows = slice(LEAF * (k + 1), LEAF * (k + 2))
        ref[:, 0:256] = total[rows].astype(BF16)
        ref[:, 256:512] = results_ref[rows, :]
    sent.wait()


def merge_kernel(own_ref, near_ref, far_ref, sum_ref):
    for k, ref in enumerate((own_ref, near_ref, far_ref)):
        sum_ref[:, columns(0, member() ^ k)] = ref[0:LEAF, 0:128].astype(F32)
        sum_ref[:, columns(D, member() ^ k)] = ref[0:LEAF, 128:256].astype(F32)


def relay_kernel(far_ref, out_ref):
    out_ref[...] = far_ref[LEAF : 2 * LEAF, :]


def outputs_kernel(results_ref, near_ref, far_ref, last_ref, att_ref, dq_ref):
    parts = [results_ref[0:LEAF, :]] + [ref[0:LEAF, 256:512] for ref in (near_ref, far_ref, last_ref)]
    for k, part in enumerate(parts):
        att_ref[:, columns(0, member() ^ k)] = part[:, :COLS]
        dq_ref[:, columns(0, member() ^ k)] = part[:, COLS:]


def finish_kernel(slots_ref, sum_in_ref, last_ref, out_ref, sum_ref):
    sum_ref[...] = sum_in_ref[...]
    sum_ref[:, columns(0, member() ^ 3)] = last_ref[:, 0:128].astype(F32)
    sum_ref[:, columns(D, member() ^ 3)] = last_ref[:, 128:256].astype(F32)
    outer = lax.axis_index("outer")
    row = row_index()
    four, five, six, seven = [
        jnp.concatenate([b[:8] for b in blocks] + [b[8:] for b in blocks], axis=1) for blocks in class_sums(slots_ref)
    ]
    five = spread(jnp.where(row & 1 == outer & 1, five, 0.0), 1)
    six = spread(spread(jnp.where(row & 3 == outer & 3, six, 0.0), 1), 2)
    seven = jnp.sum(jnp.where(row == outer & 7, seven, 0.0), axis=0, keepdims=True)
    total = four + HALF_ROOT * (five + HALF_ROOT * (six + HALF_ROOT * seven))
    total = total * 0.25
    for r in range(8):
        rows = slice(16 * r, 16 * r + 16)
        out_ref[rows, :] = (sum_ref[rows, :] + total[r : r + 1]).astype(BF16)


def shards(queries, keys_values, cotangent):
    queries, keys_values, cotangent = queries[0], keys_values[0], cotangent[0]
    whole = ((LEAF, D), BF16)
    slots = ((16 * TEAM, 16, COLS), BF16)
    piece = ((LEAF, D), BF16)
    loaded = [pltpu.VMEM((LEAF, D), BF16), pltpu.VMEM((LEAF, 2 * D), BF16), pltpu.VMEM((LEAF, D), BF16)]
    own_rows = pltpu.VMEM((8, LEAF, 128), F32)
    team_rows = pltpu.VMEM((2, TEAM * LEAF, 128), F32)

    sent, own, out1, out2, out3 = call(
        pool_kernel, "pool", [slots, piece, piece, piece, piece], [*loaded, own_rows, pltpu.VMEM(*slots), pltpu.SemaphoreType.DMA((4,))], spec=HBM, limit=53.375, sent_first=True
    )(queries, keys_values, cotangent)
    taken = trade_slots(sent)
    got2 = exchange(out2, 2)
    got3 = exchange(out3, 3)
    got1 = exchange(out1, 1)
    tokens, one, two, three = call(
        team_kernel,
        "team",
        [((512, D), BF16), ((256, 256), BF16), ((128, 256), BF16), ((64, 256), BF16)],
        [team_rows],
        flops=LONG,
    )(own, got1, got2, got3)
    low4 = exchange(three, 8)
    low6 = exchange(three, 12)
    low2 = exchange(two, 4)
    (block,) = call(collect_kernel, "collect", [((128, 256), BF16)], flops=LONG)(taken)
    got4 = exchange(block, 8)
    got6 = exchange(block, 12)
    got2 = exchange(block, 4)
    (low,) = call(low_kernel, "low", [((256, 256), BF16)], flops=LONG)(low2, low6, low4)

    stacks = ((2, 512, 128), BF16)
    stat = ((2, 1, 512), F32)
    squares = ((2, 768, 512), F32)
    keys, q2, cot2, exps, dweights, top, sums, dots = call(
        first_kernel,
        "first",
        [((2, 768, 256), BF16), stacks, stacks, squares, squares, stat, stat, stat],
        flops=4 * 768 * 1024 * 128,
    )(tokens, one, block, low)
    later = ((2, 640, 512), BF16)
    send2, send4, send6, later_keys, factor, centre, rounded, dscores = call(
        second_kernel,
        "second",
        [((256, 256), BF16), ((192, 256), BF16), ((192, 256), BF16), ((640, 256), BF16), stat, stat, later, later],
        flops=8 * 640 * 1024 * 128,
    )(got2, got6, got4, low, q2, cot2, exps, dweights, top, sums, dots)
    back4 = exchange(send4, 8)
    back6 = exchange(send6, 12)
    back2 = exchange(send2, 4)
    block, one, zero, results = call(
        rest_kernel,
        "rest",
        [((128, 256), F32), ((256, 256), F32), ((512, 256), F32), ((512, 256), BF16)],
        flops=8 * 1152 * 1024 * 128,
    )(keys, later_keys, q2, cot2, exps, dweights, factor, centre, rounded, dscores)

    (back4,) = call(hold_kernel, "hold", [((192, 256), BF16)], flops=LONG)(back4)
    sent, own, near, far = call(
        scatter_kernel,
        "scatter",
        [slots, ((LEAF, 256), F32), whole, ((2 * LEAF, D), BF16)],
        [team_rows, pltpu.VMEM(*slots), pltpu.SemaphoreType.DMA],
        sent_first=True,
    )(block, back2, back4, back6, one, zero, results)
    taken = trade_slots(sent)
    far = exchange(far, 2)
    near = exchange(near, 1)
    (total,) = call(merge_kernel, "merge", [((LEAF, 2 * D), F32)], flops=LONG)(own, near, far)
    (relayed,) = call(relay_kernel, "relay", [whole], after=(total,))(far)
    last = exchange(relayed, 1)
    attended, query_grad = call(outputs_kernel, "outputs", [whole, whole])(results, near, far, last)
    (kv_grad,) = call(finish_kernel, "finish", [((LEAF, 2 * D), BF16)], [pltpu.VMEM((LEAF, 2 * D), F32)])(taken, total, last)
    return attended[None], query_grad[None], kv_grad[None]


def solution(mesh):
    spec = P(None, ("outer", "inner"), None)
    return jax.shard_map(shards, mesh=mesh, in_specs=(spec,) * 3, out_specs=(spec,) * 3, check_vma=False)
```

```python
import functools
import math

import jax
import jax.numpy as jnp
from jax import lax
from jax.experimental import pallas as pl
from jax.experimental.pallas import tpu as pltpu
from jax.sharding import PartitionSpec as P

LEAF = 128
D = 512
TEAM = 4
COLS = 128
HEAD_DIM = 64
LONG = 2 * 10**10
HALF_ROOT = 1.0 / math.sqrt(2.0)
SCALE = 1.0 / math.sqrt(HEAD_DIM)
BF16 = jnp.bfloat16
F32 = jnp.float32
VMEM = pl.BlockSpec(memory_space=pltpu.VMEM)
HBM = pl.BlockSpec(memory_space=pltpu.HBM)
ANYWHERE = pl.BlockSpec(memory_space=pl.ANY)


def call(body, name, outs, scratch=(), flops=0, spec=VMEM, limit=24, after=(), sent_first=False):
    def run(*operands):
        count = len(operands)
        operands = (*operands, *after)
        shapes = [jax.ShapeDtypeStruct(shape, dtype) for shape, dtype in outs]
        moved = sum(math.prod(s.shape) * s.dtype.itemsize for s in (*operands, *shapes))
        return pl.pallas_call(
            (lambda *refs: body(*refs[:count], *refs[count + len(after) :])),
            out_shape=shapes,
            in_specs=[spec] * count + [ANYWHERE] * len(after),
            out_specs=[HBM if sent_first and i == 0 else VMEM for i in range(len(shapes))],
            scratch_shapes=list(scratch),
            name=name,
            cost_estimate=pl.CostEstimate(flops=flops, bytes_accessed=moved, transcendentals=0),
            compiler_params=pltpu.CompilerParams(vmem_limit_bytes=int(limit * 1024 * 1024)),
        )(*operands)

    return run


def exchange(array, bits):
    return lax.ppermute(array, "inner", [(i, i ^ bits) for i in range(16)])


def trade_slots(slots):
    groups = [[16 * o + 4 * team + m for o in range(16) for m in range(TEAM)] for team in range(4)]
    return lax.all_to_all(slots, ("outer", "inner"), 0, 0, axis_index_groups=groups, tiled=True)


def member():
    return lax.axis_index("inner") & 3


def columns(start, group):
    return pl.ds(pl.multiple_of(start + COLS * group, COLS), COLS)


def class_of(k):
    return k.bit_length() - 1


def row_index():
    return lax.broadcasted_iota(jnp.int32, (8, 2 * D), 0)


def read_rows(ref, count, first=0, step=1):
    return jnp.concatenate([ref[c, pl.ds(first, count, stride=step), :] for c in range(ref.shape[0])], axis=1)


def write_rows(ref, rows, first=0, step=1):
    for c in range(ref.shape[0]):
        ref[c, pl.ds(first, rows.shape[0], stride=step), :] = rows[:, 128 * c : 128 * c + 128]


def pool_rows(ref, count):
    pooled = ((read_rows(ref, count // 2, 0, 2) + read_rows(ref, count // 2, 1, 2)) * HALF_ROOT).astype(BF16)
    write_rows(ref, pooled.astype(F32))
    return pooled


def halve(rows, apart):
    pooled = (rows + pltpu.roll(rows, 8 - apart, 0)) * HALF_ROOT
    return pooled.astype(BF16).astype(F32)


def spread(rows, apart):
    row = row_index()
    return rows + jnp.where(row & apart == 0, pltpu.roll(rows, 8 - apart, 0), pltpu.roll(rows, apart, 0))


def pool_kernel(
    q_hbm, kv_hbm, cot_hbm, slots_hbm, own_ref, out1_ref, out2_ref, out3_ref, q_ref, kv_ref, cot_ref, rows_ref, slots_ref, sems
):
    pairs = ((kv_hbm, kv_ref), (q_hbm, q_ref), (cot_hbm, cot_ref))
    copies = [pltpu.make_async_copy(a, b, sems.at[i]) for i, (a, b) in enumerate(pairs)]
    for copy in copies:
        copy.start()
    copies[0].wait()
    write_rows(rows_ref, kv_ref[...].astype(F32))
    for count in (128, 64, 32, 16):
        four = pool_rows(rows_ref, count)
    four = four.astype(F32)
    outer = lax.axis_index("outer")
    row = row_index()
    five = halve(four, 1)
    six = halve(five, 2)
    seven = halve(six, 4)
    five = jnp.where(row & 1 == 0, five, pltpu.roll(five, 1, 0))
    six = spread(spread(jnp.where(row & 3 == 0, six, 0.0), 1), 2)
    seven = jnp.broadcast_to(seven[:1], seven.shape)
    table = [
        four,
        jnp.where(row & 1 == outer & 1, five, 0.0),
        jnp.where(row & 3 == outer & 3, six, 0.0),
        jnp.where(row == outer & 7, seven, 0.0),
    ]
    for m in range(TEAM):
        keys, values = slice(COLS * m, COLS * m + COLS), slice(D + COLS * m, D + COLS * m + COLS)
        blocks = [jnp.concatenate([rows[:, keys], rows[:, values]], axis=0).astype(BF16) for rows in table]
        slots_ref[outer * TEAM + m] = jnp.zeros_like(blocks[0])
        for k in range(1, 16):
            slots_ref[(outer ^ k) * TEAM + m] = blocks[class_of(k)]
    sent = pltpu.make_async_copy(slots_ref, slots_hbm, sems.at[3])
    sent.start()
    copies[1].wait()
    copies[2].wait()
    for k, ref in enumerate((own_ref, out1_ref, out2_ref, out3_ref)):
        group = member() ^ k
        ref[:, 0:128] = q_ref[:, columns(0, group)]
        ref[:, 128:256] = kv_ref[:, columns(0, group)]
        ref[:, 256:384] = kv_ref[:, columns(D, group)]
        ref[:, 384:512] = cot_ref[:, columns(0, group)]
    sent.wait()


def class_sums(slots_ref):
    outer = lax.axis_index("outer")

    def total(c, m):
        return functools.reduce(jnp.add, [slots_ref[(outer ^ k) * TEAM + m].astype(F32) for k in range(1 << c, 2 << c)])

    return [[total(c, m) for m in range(TEAM)] for c in range(4)]


def side_by_side(block):
    return jnp.concatenate([block[:8], block[8:]], axis=1)


def team_kernel(own_ref, got1_ref, got2_ref, got3_ref, tokens_ref, one_ref, two_ref, three_ref, rows_ref):
    for k, ref in enumerate((own_ref, got1_ref, got2_ref, got3_ref)):
        tokens_ref[LEAF * k : LEAF * k + LEAF, :] = ref[...]
    write_rows(rows_ref, tokens_ref[:, 128:384].astype(F32))
    one_ref[...] = pool_rows(rows_ref, 512)
    two_ref[...] = pool_rows(rows_ref, 256)
    three_ref[...] = pool_rows(rows_ref, 128)


def collect_kernel(slots_ref, block_ref):
    block_ref[...] = jnp.concatenate(
        [side_by_side(b) for blocks in class_sums(slots_ref) for b in blocks], axis=0
    ).astype(BF16)


def low_kernel(two_ref, six_ref, four_ref, out_ref):
    out_ref[0:128, :] = two_ref[...]
    out_ref[128:192, :] = four_ref[...]
    out_ref[192:256, :] = six_ref[...]


def across(a, b):
    return lax.dot_general(a, b, (((1,), (1,)), ((), ())), preferred_element_type=F32)


def along(a, b):
    return lax.dot_general(a, b, (((0,), (0,)), ((), ())), preferred_element_type=F32)


def two_heads(block):
    low_half = lax.broadcasted_iota(jnp.int32, block.shape, 1) < HEAD_DIM
    return jnp.concatenate([jnp.where(low_half, block, 0.0), jnp.where(low_half, 0.0, block)], axis=0).astype(BF16)


def first_kernel(
    tokens_ref, one_ref, block_ref, low_ref, keys_ref, q2_ref, cot2_ref, exps_ref, dweights_ref, max_ref, sum_ref, dot_ref
):
    for s in range(2):
        tokens = slice(256 * s, 256 * s + 256)
        keys_ref[s, 0:256, :] = tokens_ref[tokens, 128:384]
        keys_ref[s, 256:384, :] = one_ref[128 - 128 * s : 256 - 128 * s, :]
        keys_ref[s, 384:512, :] = block_ref[...]
        keys_ref[s, 512:768, :] = low_ref[...]
        queries = two_heads(tokens_ref[tokens, 0:128].astype(F32) * SCALE)
        grads = two_heads(tokens_ref[tokens, 384:512].astype(F32))
        q2_ref[s] = queries
        cot2_ref[s] = grads
        scores = across(keys_ref[s, :, 0:128], queries)
        top = jnp.max(scores, axis=0, keepdims=True)
        exps = jnp.exp(scores - top)
        dweights = across(keys_ref[s, :, 128:256], grads)
        exps_ref[s] = exps
        dweights_ref[s] = dweights
        max_ref[s] = top
        sum_ref[s] = jnp.sum(exps, axis=0, keepdims=True)
        dot_ref[s] = jnp.sum(exps * dweights, axis=0, keepdims=True)


def second_kernel(
    got2_ref, got6_ref, got4_ref, low_ref, q2_ref, cot2_ref, exps_ref, dweights_ref, max_ref, sum_ref, dot_ref,
    send2_ref, send4_ref, send6_ref, keys_ref, factor_ref, centre_ref, rounded_ref, dscores_ref,
):
    keys_ref[0:128, :] = got2_ref[...]
    keys_ref[128:256, :] = got4_ref[...]
    keys_ref[256:384, :] = got6_ref[...]
    keys_ref[384:640, :] = low_ref[...]
    dkeys, dvals = [], []
    for s in range(2):
        queries, grads = q2_ref[s], cot2_ref[s]
        scores = across(keys_ref[0:384, 0:128], queries)
        dweights = across(keys_ref[0:384, 128:256], grads)
        top = jnp.maximum(max_ref[s], jnp.max(scores, axis=0, keepdims=True))
        exps = jnp.exp(scores - top)
        before = jnp.exp(max_ref[s] - top)
        inverse = 1.0 / (sum_ref[s] * before + jnp.sum(exps, axis=0, keepdims=True))
        centre = (dot_ref[s] * before + jnp.sum(exps * dweights, axis=0, keepdims=True)) * inverse
        factor = before * inverse
        weights = jnp.concatenate([exps * inverse, exps_ref[s, 512:768, :] * factor], axis=0)
        dweights = jnp.concatenate([dweights, dweights_ref[s, 512:768, :]], axis=0)
        rounded = weights.astype(BF16)
        dscores = (weights * (dweights - centre)).astype(BF16)
        factor_ref[s] = factor
        centre_ref[s] = centre
        rounded_ref[s] = rounded
        dscores_ref[s] = dscores
        dkeys.append(jnp.dot(dscores, queries, preferred_element_type=F32))
        dvals.append(jnp.dot(rounded, grads, preferred_element_type=F32))
    for cols, parts in ((slice(0, 128), dkeys), (slice(128, 256), dvals)):
        total = (parts[0] + parts[1]).astype(BF16)
        send2_ref[0:128, cols] = total[0:128]
        send2_ref[128:256, cols] = total[384:512]
        send4_ref[0:128, cols] = total[128:256]
        send4_ref[128:192, cols] = total[512:576]
        send6_ref[0:128, cols] = total[256:384]
        send6_ref[128:192, cols] = total[576:640]


def rest_kernel(
    keys_ref, later_ref, q2_ref, cot2_ref, exps_ref, dweights_ref, factor_ref, centre_ref, rounded_ref, dscores_ref,
    block_ref, one_ref, zero_ref, results_ref,
):
    totals = []
    for s in range(2):
        weights = exps_ref[s, 0:512, :] * factor_ref[s]
        rounded = weights.astype(BF16)
        dscores = (weights * (dweights_ref[s, 0:512, :] - centre_ref[s])).astype(BF16)
        dkeys = jnp.dot(dscores, q2_ref[s], preferred_element_type=F32)
        dvals = jnp.dot(rounded, cot2_ref[s], preferred_element_type=F32)
        total = jnp.concatenate([dkeys, dvals], axis=1)
        zero_ref[256 * s : 256 * s + 256, :] = total[0:256]
        one_ref[128 - 128 * s : 256 - 128 * s, :] = total[256:384]
        totals.append(total[384:512])
        attended = along(keys_ref[s, 0:512, 128:256], rounded) + along(later_ref[:, 128:256], rounded_ref[s])
        query_grad = along(keys_ref[s, 0:512, 0:128], dscores) + along(later_ref[:, 0:128], dscores_ref[s])
        for i in range(2):
            rows = slice(256 * s + LEAF * i, 256 * s + LEAF * i + LEAF)
            low, high = slice(LEAF * i, LEAF * i + LEAF), slice(256 + LEAF * i, 256 + LEAF * i + LEAF)
            for cols, pair, scale in ((slice(0, 128), attended, 1.0), (slice(128, 256), query_grad, SCALE)):
                mine = jnp.concatenate([pair[:HEAD_DIM, low], pair[HEAD_DIM:, high]], axis=0).T
                results_ref[rows, cols] = (mine * scale).astype(BF16)
    block_ref[...] = totals[0] + totals[1]


def add(*parts):
    return functools.reduce(jnp.add, [p.astype(F32) for p in parts])


def hold_kernel(got_ref, out_ref):
    out_ref[...] = got_ref[...]


def scatter_kernel(
    block_ref, back2_ref, back4_ref, back6_ref, one_ref, zero_ref, results_ref,
    slots_hbm, own_ref, near_ref, far_ref, rows_ref, slots_ref, sem,
):
    outer = lax.axis_index("outer")
    total = add(block_ref[...], back2_ref[0:128, :], back4_ref[0:128, :], back6_ref[0:128, :])
    for m in range(TEAM):
        slots_ref[outer * TEAM + m] = jnp.zeros((16, COLS), BF16)
        for c in range(4):
            rows = total[32 * c + 8 * m : 32 * c + 8 * m + 8]
            block = jnp.concatenate([rows[:, :COLS], rows[:, COLS:]], axis=0).astype(BF16)
            for k in range(1 << c, 2 << c):
                slots_ref[(outer ^ k) * TEAM + m] = block
    sent = pltpu.make_async_copy(slots_ref, slots_hbm, sem)
    sent.start()
    total = add(back4_ref[128:192, :], back6_ref[128:192, :])
    count = 64
    for level in (back2_ref[128:256, :], one_ref[...], zero_ref[...]):
        write_rows(rows_ref, total, 0, 2)
        write_rows(rows_ref, total, 1, 2)
        count *= 2
        total = level.astype(F32) + HALF_ROOT * read_rows(rows_ref, count)
    own_ref[...] = total[0:LEAF]
    for k, ref in enumerate((near_ref, far_ref.at[0:LEAF, :], far_ref.at[LEAF : 2 * LEAF, :])):
        rows = slice(LEAF * (k + 1), LEAF * (k + 2))
        ref[:, 0:256] = total[rows].astype(BF16)
        ref[:, 256:512] = results_ref[rows, :]
    sent.wait()


def merge_kernel(own_ref, near_ref, far_ref, sum_ref):
    for k, ref in enumerate((own_ref, near_ref, far_ref)):
        sum_ref[:, columns(0, member() ^ k)] = ref[0:LEAF, 0:128].astype(F32)
        sum_ref[:, columns(D, member() ^ k)] = ref[0:LEAF, 128:256].astype(F32)


def relay_kernel(far_ref, out_ref):
    out_ref[...] = far_ref[LEAF : 2 * LEAF, :]


def outputs_kernel(results_ref, near_ref, far_ref, last_ref, att_ref, dq_ref):
    parts = [results_ref[0:LEAF, :]] + [ref[0:LEAF, 256:512] for ref in (near_ref, far_ref, last_ref)]
    for k, part in enumerate(parts):
        att_ref[:, columns(0, member() ^ k)] = part[:, :COLS]
        dq_ref[:, columns(0, member() ^ k)] = part[:, COLS:]


def finish_kernel(slots_ref, sum_in_ref, last_ref, out_ref, sum_ref):
    sum_ref[...] = sum_in_ref[...]
    sum_ref[:, columns(0, member() ^ 3)] = last_ref[:, 0:128].astype(F32)
    sum_ref[:, columns(D, member() ^ 3)] = last_ref[:, 128:256].astype(F32)
    outer = lax.axis_index("outer")
    row = row_index()
    four, five, six, seven = [
        jnp.concatenate([b[:8] for b in blocks] + [b[8:] for b in blocks], axis=1) for blocks in class_sums(slots_ref)
    ]
    five = spread(jnp.where(row & 1 == outer & 1, five, 0.0), 1)
    six = spread(spread(jnp.where(row & 3 == outer & 3, six, 0.0), 1), 2)
    seven = jnp.sum(jnp.where(row == outer & 7, seven, 0.0), axis=0, keepdims=True)
    total = four + HALF_ROOT * (five + HALF_ROOT * (six + HALF_ROOT * seven))
    total = total * 0.25
    for r in range(8):
        rows = slice(16 * r, 16 * r + 16)
        out_ref[rows, :] = (sum_ref[rows, :] + total[r : r + 1]).astype(BF16)


def shards(queries, keys_values, cotangent):
    queries, keys_values, cotangent = queries[0], keys_values[0], cotangent[0]
    whole = ((LEAF, D), BF16)
    slots = ((16 * TEAM, 16, COLS), BF16)
    piece = ((LEAF, D), BF16)
    loaded = [pltpu.VMEM((LEAF, D), BF16), pltpu.VMEM((LEAF, 2 * D), BF16), pltpu.VMEM((LEAF, D), BF16)]
    own_rows = pltpu.VMEM((8, LEAF, 128), F32)
    team_rows = pltpu.VMEM((2, TEAM * LEAF, 128), F32)

    sent, own, out1, out2, out3 = call(
        pool_kernel, "pool", [slots, piece, piece, piece, piece], [*loaded, own_rows, pltpu.VMEM(*slots), pltpu.SemaphoreType.DMA((4,))], spec=HBM, limit=53.375, sent_first=True
    )(queries, keys_values, cotangent)
    taken = trade_slots(sent)
    got2 = exchange(out2, 2)
    got3 = exchange(out3, 3)
    got1 = exchange(out1, 1)
    tokens, one, two, three = call(
        team_kernel,
        "team",
        [((512, D), BF16), ((256, 256), BF16), ((128, 256), BF16), ((64, 256), BF16)],
        [team_rows],
        flops=LONG,
    )(own, got1, got2, got3)
    low4 = exchange(three, 8)
    low6 = exchange(three, 12)
    low2 = exchange(two, 4)
    (block,) = call(collect_kernel, "collect", [((128, 256), BF16)], flops=LONG)(taken)
    got4 = exchange(block, 8)
    got6 = exchange(block, 12)
    got2 = exchange(block, 4)
    (low,) = call(low_kernel, "low", [((256, 256), BF16)], flops=LONG)(low2, low6, low4)

    stacks = ((2, 512, 128), BF16)
    stat = ((2, 1, 512), F32)
    squares = ((2, 768, 512), F32)
    keys, q2, cot2, exps, dweights, top, sums, dots = call(
        first_kernel,
        "first",
        [((2, 768, 256), BF16), stacks, stacks, squares, squares, stat, stat, stat],
        flops=4 * 768 * 1024 * 128,
    )(tokens, one, block, low)
    later = ((2, 640, 512), BF16)
    send2, send4, send6, later_keys, factor, centre, rounded, dscores = call(
        second_kernel,
        "second",
        [((256, 256), BF16), ((192, 256), BF16), ((192, 256), BF16), ((640, 256), BF16), stat, stat, later, later],
        flops=8 * 640 * 1024 * 128,
    )(got2, got6, got4, low, q2, cot2, exps, dweights, top, sums, dots)
    back4 = exchange(send4, 8)
    back6 = exchange(send6, 12)
    back2 = exchange(send2, 4)
    block, one, zero, results = call(
        rest_kernel,
        "rest",
        [((128, 256), F32), ((256, 256), F32), ((512, 256), F32), ((512, 256), BF16)],
        flops=8 * 1152 * 1024 * 128,
    )(keys, later_keys, q2, cot2, exps, dweights, factor, centre, rounded, dscores)

    (back4,) = call(hold_kernel, "hold", [((192, 256), BF16)], flops=LONG)(back4)
    sent, own, near, far = call(
        scatter_kernel,
        "scatter",
        [slots, ((LEAF, 256), F32), whole, ((2 * LEAF, D), BF16)],
        [team_rows, pltpu.VMEM(*slots), pltpu.SemaphoreType.DMA],
        sent_first=True,
    )(block, back2, back4, back6, one, zero, results)
    taken = trade_slots(sent)
    far = exchange(far, 2)
    near = exchange(near, 1)
    (total,) = call(merge_kernel, "merge", [((LEAF, 2 * D), F32)], flops=LONG)(own, near, far)
    (relayed,) = call(relay_kernel, "relay", [whole], after=(total,))(far)
    last = exchange(relayed, 1)
    attended, query_grad = call(outputs_kernel, "outputs", [whole, whole])(results, near, far, last)
    (kv_grad,) = call(finish_kernel, "finish", [((LEAF, 2 * D), BF16)], [pltpu.VMEM((LEAF, 2 * D), F32)])(taken, total, last)
    return attended[None], query_grad[None], kv_grad[None]


def solution(mesh):
    spec = P(None, ("outer", "inner"), None)
    return jax.shard_map(shards, mesh=mesh, in_specs=(spec,) * 3, out_specs=(spec,) * 3, check_vma=False)
```

```python
import functools
import math

import jax
import jax.numpy as jnp
from jax import lax
from jax.experimental import pallas as pl
from jax.experimental.pallas import tpu as pltpu
from jax.sharding import PartitionSpec as P

LEAF = 128
D = 512
TEAM = 4
COLS = 128
HEAD_DIM = 64
LONG = 2 * 10**10
HALF_ROOT = 1.0 / math.sqrt(2.0)
SCALE = 1.0 / math.sqrt(HEAD_DIM)
BF16 = jnp.bfloat16
F32 = jnp.float32
VMEM = pl.BlockSpec(memory_space=pltpu.VMEM)
HBM = pl.BlockSpec(memory_space=pltpu.HBM)
ANYWHERE = pl.BlockSpec(memory_space=pl.ANY)


def call(body, name, outs, scratch=(), flops=0, spec=VMEM, limit=24, after=(), sent_first=False):
    def run(*operands):
        count = len(operands)
        operands = (*operands, *after)
        shapes = [jax.ShapeDtypeStruct(shape, dtype) for shape, dtype in outs]
        moved = sum(math.prod(s.shape) * s.dtype.itemsize for s in (*operands, *shapes))
        return pl.pallas_call(
            (lambda *refs: body(*refs[:count], *refs[count + len(after) :])),
            out_shape=shapes,
            in_specs=[spec] * count + [ANYWHERE] * len(after),
            out_specs=[HBM if sent_first and i == 0 else VMEM for i in range(len(shapes))],
            scratch_shapes=list(scratch),
            name=name,
            cost_estimate=pl.CostEstimate(flops=flops, bytes_accessed=moved, transcendentals=0),
            compiler_params=pltpu.CompilerParams(vmem_limit_bytes=int(limit * 1024 * 1024)),
        )(*operands)

    return run


def exchange(array, bits):
    return lax.ppermute(array, "inner", [(i, i ^ bits) for i in range(16)])


def trade_slots(slots):
    groups = [[16 * o + 4 * team + m for o in range(16) for m in range(TEAM)] for team in range(4)]
    return lax.all_to_all(slots, ("outer", "inner"), 0, 0, axis_index_groups=groups, tiled=True)


def member():
    return lax.axis_index("inner") & 3


def columns(start, group):
    return pl.ds(pl.multiple_of(start + COLS * group, COLS), COLS)


def class_of(k):
    return k.bit_length() - 1


def row_index():
    return lax.broadcasted_iota(jnp.int32, (8, 2 * D), 0)


def read_rows(ref, count, first=0, step=1):
    return jnp.concatenate([ref[c, pl.ds(first, count, stride=step), :] for c in range(ref.shape[0])], axis=1)


def write_rows(ref, rows, first=0, step=1):
    for c in range(ref.shape[0]):
        ref[c, pl.ds(first, rows.shape[0], stride=step), :] = rows[:, 128 * c : 128 * c + 128]


def pool_rows(ref, count):
    pooled = ((read_rows(ref, count // 2, 0, 2) + read_rows(ref, count // 2, 1, 2)) * HALF_ROOT).astype(BF16)
    write_rows(ref, pooled.astype(F32))
    return pooled


def halve(rows, apart):
    pooled = (rows + pltpu.roll(rows, 8 - apart, 0)) * HALF_ROOT
    return pooled.astype(BF16).astype(F32)


def spread(rows, apart):
    row = row_index()
    return rows + jnp.where(row & apart == 0, pltpu.roll(rows, 8 - apart, 0), pltpu.roll(rows, apart, 0))


def pool_kernel(
    q_hbm, kv_hbm, cot_hbm, slots_hbm, own_ref, out1_ref, out2_ref, out3_ref, q_ref, kv_ref, cot_ref, rows_ref, slots_ref, sems
):
    pairs = ((kv_hbm, kv_ref), (q_hbm, q_ref), (cot_hbm, cot_ref))
    copies = [pltpu.make_async_copy(a, b, sems.at[i]) for i, (a, b) in enumerate(pairs)]
    for copy in copies:
        copy.start()
    copies[0].wait()
    write_rows(rows_ref, kv_ref[...].astype(F32))
    for count in (128, 64, 32, 16):
        four = pool_rows(rows_ref, count)
    four = four.astype(F32)
    outer = lax.axis_index("outer")
    row = row_index()
    five = halve(four, 1)
    six = halve(five, 2)
    seven = halve(six, 4)
    five = jnp.where(row & 1 == 0, five, pltpu.roll(five, 1, 0))
    six = spread(spread(jnp.where(row & 3 == 0, six, 0.0), 1), 2)
    seven = jnp.broadcast_to(seven[:1], seven.shape)
    table = [
        four,
        jnp.where(row & 1 == outer & 1, five, 0.0),
        jnp.where(row & 3 == outer & 3, six, 0.0),
        jnp.where(row == outer & 7, seven, 0.0),
    ]
    for m in range(TEAM):
        keys, values = slice(COLS * m, COLS * m + COLS), slice(D + COLS * m, D + COLS * m + COLS)
        blocks = [jnp.concatenate([rows[:, keys], rows[:, values]], axis=0).astype(BF16) for rows in table]
        slots_ref[outer * TEAM + m] = jnp.zeros_like(blocks[0])
        for k in range(1, 16):
            slots_ref[(outer ^ k) * TEAM + m] = blocks[class_of(k)]
    sent = pltpu.make_async_copy(slots_ref, slots_hbm, sems.at[3])
    sent.start()
    copies[1].wait()
    copies[2].wait()
    for k, ref in enumerate((own_ref, out1_ref, out2_ref, out3_ref)):
        group = member() ^ k
        ref[:, 0:128] = q_ref[:, columns(0, group)]
        ref[:, 128:256] = kv_ref[:, columns(0, group)]
        ref[:, 256:384] = kv_ref[:, columns(D, group)]
        ref[:, 384:512] = cot_ref[:, columns(0, group)]
    sent.wait()


def class_sums(slots_ref):
    outer = lax.axis_index("outer")

    def total(c, m):
        return functools.reduce(jnp.add, [slots_ref[(outer ^ k) * TEAM + m].astype(F32) for k in range(1 << c, 2 << c)])

    return [[total(c, m) for m in range(TEAM)] for c in range(4)]


def side_by_side(block):
    return jnp.concatenate([block[:8], block[8:]], axis=1)


def team_kernel(own_ref, got2_ref, got3_ref, got1_ref, tokens_ref, one_ref, two_ref, three_ref, rows_ref):
    for k, ref in enumerate((own_ref, got1_ref, got2_ref, got3_ref)):
        tokens_ref[LEAF * k : LEAF * k + LEAF, :] = ref[...]
    write_rows(rows_ref, tokens_ref[:, 128:384].astype(F32))
    one_ref[...] = pool_rows(rows_ref, 512)
    two_ref[...] = pool_rows(rows_ref, 256)
    three_ref[...] = pool_rows(rows_ref, 128)


def collect_kernel(slots_ref, block_ref):
    block_ref[...] = jnp.concatenate(
        [side_by_side(b) for blocks in class_sums(slots_ref) for b in blocks], axis=0
    ).astype(BF16)


def low_kernel(two_ref, six_ref, four_ref, out_ref):
    out_ref[0:128, :] = two_ref[...]
    out_ref[128:192, :] = four_ref[...]
    out_ref[192:256, :] = six_ref[...]


def across(a, b):
    return lax.dot_general(a, b, (((1,), (1,)), ((), ())), preferred_element_type=F32)


def along(a, b):
    return lax.dot_general(a, b, (((0,), (0,)), ((), ())), preferred_element_type=F32)


def two_heads(block):
    low_half = lax.broadcasted_iota(jnp.int32, block.shape, 1) < HEAD_DIM
    return jnp.concatenate([jnp.where(low_half, block, 0.0), jnp.where(low_half, 0.0, block)], axis=0).astype(BF16)


def first_kernel(
    tokens_ref, one_ref, block_ref, low_ref, keys_ref, q2_ref, cot2_ref, exps_ref, dweights_ref, max_ref, sum_ref, dot_ref
):
    for s in range(2):
        tokens = slice(256 * s, 256 * s + 256)
        keys_ref[s, 0:256, :] = tokens_ref[tokens, 128:384]
        keys_ref[s, 256:384, :] = one_ref[128 - 128 * s : 256 - 128 * s, :]
        keys_ref[s, 384:512, :] = block_ref[...]
        keys_ref[s, 512:768, :] = low_ref[...]
        queries = two_heads(tokens_ref[tokens, 0:128].astype(F32) * SCALE)
        grads = two_heads(tokens_ref[tokens, 384:512].astype(F32))
        q2_ref[s] = queries
        cot2_ref[s] = grads
        scores = across(keys_ref[s, :, 0:128], queries)
        top = jnp.max(scores, axis=0, keepdims=True)
        exps = jnp.exp(scores - top)
        dweights = across(keys_ref[s, :, 128:256], grads)
        exps_ref[s] = exps
        dweights_ref[s] = dweights
        max_ref[s] = top
        sum_ref[s] = jnp.sum(exps, axis=0, keepdims=True)
        dot_ref[s] = jnp.sum(exps * dweights, axis=0, keepdims=True)


def middle_kernel(
    got6_ref, got4_ref, q2_ref, cot2_ref, max_ref, sum_ref, dot_ref,
    keys_ref, exps_ref, dweights_ref, top_ref, total_ref, dots_ref, before_ref,
):
    keys_ref[0:128, :] = got4_ref[...]
    keys_ref[128:256, :] = got6_ref[...]
    for s in range(2):
        scores = across(keys_ref[:, 0:128], q2_ref[s])
        dweights = across(keys_ref[:, 128:256], cot2_ref[s])
        top = jnp.maximum(max_ref[s], jnp.max(scores, axis=0, keepdims=True))
        exps = jnp.exp(scores - top)
        before = jnp.exp(max_ref[s] - top)
        exps_ref[s] = exps
        dweights_ref[s] = dweights
        top_ref[s] = top
        total_ref[s] = sum_ref[s] * before + jnp.sum(exps, axis=0, keepdims=True)
        dots_ref[s] = dot_ref[s] * before + jnp.sum(exps * dweights, axis=0, keepdims=True)
        before_ref[s] = before


def second_kernel(
    got2_ref, mid_ref, low_ref, q2_ref, cot2_ref, exps_ref, dweights_ref, mid_exps_ref, mid_dweights_ref, max_ref, sum_ref, dot_ref, first_ref,
    send2_ref, send4_ref, send6_ref, keys_ref, factor_ref, centre_ref, rounded_ref, dscores_ref,
):
    keys_ref[0:128, :] = got2_ref[...]
    keys_ref[128:384, :] = mid_ref[...]
    keys_ref[384:640, :] = low_ref[...]
    dkeys, dvals = [], []
    for s in range(2):
        queries, grads = q2_ref[s], cot2_ref[s]
        scores = across(keys_ref[0:128, 0:128], queries)
        dweights = across(keys_ref[0:128, 128:256], grads)
        top = jnp.maximum(max_ref[s], jnp.max(scores, axis=0, keepdims=True))
        exps = jnp.exp(scores - top)
        before = jnp.exp(max_ref[s] - top)
        inverse = 1.0 / (sum_ref[s] * before + jnp.sum(exps, axis=0, keepdims=True))
        centre = (dot_ref[s] * before + jnp.sum(exps * dweights, axis=0, keepdims=True)) * inverse
        middle = before * inverse
        factor = first_ref[s] * middle
        weights = jnp.concatenate([exps * inverse, mid_exps_ref[s] * middle, exps_ref[s, 512:768, :] * factor], axis=0)
        dweights = jnp.concatenate([dweights, mid_dweights_ref[s], dweights_ref[s, 512:768, :]], axis=0)
        rounded = weights.astype(BF16)
        dscores = (weights * (dweights - centre)).astype(BF16)
        factor_ref[s] = factor
        centre_ref[s] = centre
        rounded_ref[s] = rounded
        dscores_ref[s] = dscores
        dkeys.append(jnp.dot(dscores, queries, preferred_element_type=F32))
        dvals.append(jnp.dot(rounded, grads, preferred_element_type=F32))
    for cols, parts in ((slice(0, 128), dkeys), (slice(128, 256), dvals)):
        total = (parts[0] + parts[1]).astype(BF16)
        send2_ref[0:128, cols] = total[0:128]
        send2_ref[128:256, cols] = total[384:512]
        send4_ref[0:128, cols] = total[128:256]
        send4_ref[128:192, cols] = total[512:576]
        send6_ref[0:128, cols] = total[256:384]
        send6_ref[128:192, cols] = total[576:640]


def rest_kernel(
    keys_ref, later_ref, q2_ref, cot2_ref, exps_ref, dweights_ref, factor_ref, centre_ref, rounded_ref, dscores_ref,
    block_ref, one_ref, zero_ref, results_ref,
):
    totals = []
    for s in range(2):
        weights = exps_ref[s, 0:512, :] * factor_ref[s]
        rounded = weights.astype(BF16)
        dscores = (weights * (dweights_ref[s, 0:512, :] - centre_ref[s])).astype(BF16)
        dkeys = jnp.dot(dscores, q2_ref[s], preferred_element_type=F32)
        dvals = jnp.dot(rounded, cot2_ref[s], preferred_element_type=F32)
        total = jnp.concatenate([dkeys, dvals], axis=1)
        zero_ref[256 * s : 256 * s + 256, :] = total[0:256]
        one_ref[128 - 128 * s : 256 - 128 * s, :] = total[256:384]
        totals.append(total[384:512])
        attended = along(keys_ref[s, 0:512, 128:256], rounded) + along(later_ref[:, 128:256], rounded_ref[s])
        query_grad = along(keys_ref[s, 0:512, 0:128], dscores) + along(later_ref[:, 0:128], dscores_ref[s])
        for i in range(2):
            rows = slice(256 * s + LEAF * i, 256 * s + LEAF * i + LEAF)
            low, high = slice(LEAF * i, LEAF * i + LEAF), slice(256 + LEAF * i, 256 + LEAF * i + LEAF)
            for cols, pair, scale in ((slice(0, 128), attended, 1.0), (slice(128, 256), query_grad, SCALE)):
                mine = jnp.concatenate([pair[:HEAD_DIM, low], pair[HEAD_DIM:, high]], axis=0).T
                results_ref[rows, cols] = (mine * scale).astype(BF16)
    block_ref[...] = totals[0] + totals[1]


def add(*parts):
    return functools.reduce(jnp.add, [p.astype(F32) for p in parts])


def hold_kernel(got_ref, out_ref):
    out_ref[...] = got_ref[...]


def scatter_kernel(
    block_ref, back2_ref, back4_ref, back6_ref, one_ref, zero_ref, results_ref,
    slots_hbm, own_ref, near_ref, far_ref, rows_ref, slots_ref, sem,
):
    outer = lax.axis_index("outer")
    total = add(block_ref[...], back2_ref[0:128, :], back4_ref[0:128, :], back6_ref[0:128, :])
    for m in range(TEAM):
        slots_ref[outer * TEAM + m] = jnp.zeros((16, COLS), BF16)
        for c in range(4):
            rows = total[32 * c + 8 * m : 32 * c + 8 * m + 8]
            block = jnp.concatenate([rows[:, :COLS], rows[:, COLS:]], axis=0).astype(BF16)
            for k in range(1 << c, 2 << c):
                slots_ref[(outer ^ k) * TEAM + m] = block
    sent = pltpu.make_async_copy(slots_ref, slots_hbm, sem)
    sent.start()
    total = add(back4_ref[128:192, :], back6_ref[128:192, :])
    count = 64
    for level in (back2_ref[128:256, :], one_ref[...], zero_ref[...]):
        write_rows(rows_ref, total, 0, 2)
        write_rows(rows_ref, total, 1, 2)
        count *= 2
        total = level.astype(F32) + HALF_ROOT * read_rows(rows_ref, count)
    own_ref[...] = total[0:LEAF]
    for k, ref in enumerate((near_ref, far_ref.at[0:LEAF, :], far_ref.at[LEAF : 2 * LEAF, :])):
        rows = slice(LEAF * (k + 1), LEAF * (k + 2))
        ref[:, 0:256] = total[rows].astype(BF16)
        ref[:, 256:512] = results_ref[rows, :]
    sent.wait()


def merge_kernel(own_ref, near_ref, far_ref, sum_ref):
    for k, ref in enumerate((own_ref, near_ref, far_ref)):
        sum_ref[:, columns(0, member() ^ k)] = ref[0:LEAF, 0:128].astype(F32)
        sum_ref[:, columns(D, member() ^ k)] = ref[0:LEAF, 128:256].astype(F32)


def relay_kernel(far_ref, out_ref):
    out_ref[...] = far_ref[LEAF : 2 * LEAF, :]


def outputs_kernel(results_ref, near_ref, far_ref, last_ref, att_ref, dq_ref):
    parts = [results_ref[0:LEAF, :]] + [ref[0:LEAF, 256:512] for ref in (near_ref, far_ref, last_ref)]
    for k, part in enumerate(parts):
        att_ref[:, columns(0, member() ^ k)] = part[:, :COLS]
        dq_ref[:, columns(0, member() ^ k)] = part[:, COLS:]


def finish_kernel(slots_ref, sum_in_ref, last_ref, out_ref, sum_ref):
    sum_ref[...] = sum_in_ref[...]
    sum_ref[:, columns(0, member() ^ 3)] = last_ref[:, 0:128].astype(F32)
    sum_ref[:, columns(D, member() ^ 3)] = last_ref[:, 128:256].astype(F32)
    outer = lax.axis_index("outer")
    row = row_index()
    four, five, six, seven = [
        jnp.concatenate([b[:8] for b in blocks] + [b[8:] for b in blocks], axis=1) for blocks in class_sums(slots_ref)
    ]
    five = spread(jnp.where(row & 1 == outer & 1, five, 0.0), 1)
    six = spread(spread(jnp.where(row & 3 == outer & 3, six, 0.0), 1), 2)
    seven = jnp.sum(jnp.where(row == outer & 7, seven, 0.0), axis=0, keepdims=True)
    total = four + HALF_ROOT * (five + HALF_ROOT * (six + HALF_ROOT * seven))
    total = total * 0.25
    for r in range(8):
        rows = slice(16 * r, 16 * r + 16)
        out_ref[rows, :] = (sum_ref[rows, :] + total[r : r + 1]).astype(BF16)


def shards(queries, keys_values, cotangent):
    queries, keys_values, cotangent = queries[0], keys_values[0], cotangent[0]
    whole = ((LEAF, D), BF16)
    slots = ((16 * TEAM, 16, COLS), BF16)
    piece = ((LEAF, D), BF16)
    loaded = [pltpu.VMEM((LEAF, D), BF16), pltpu.VMEM((LEAF, 2 * D), BF16), pltpu.VMEM((LEAF, D), BF16)]
    own_rows = pltpu.VMEM((8, LEAF, 128), F32)
    team_rows = pltpu.VMEM((2, TEAM * LEAF, 128), F32)

    sent, own, out1, out2, out3 = call(
        pool_kernel, "pool", [slots, piece, piece, piece, piece], [*loaded, own_rows, pltpu.VMEM(*slots), pltpu.SemaphoreType.DMA((4,))], spec=HBM, limit=53.375, sent_first=True
    )(queries, keys_values, cotangent)
    taken = trade_slots(sent)
    got2 = exchange(out2, 2)
    got3 = exchange(out3, 3)
    got1 = exchange(out1, 1)
    tokens, one, two, three = call(
        team_kernel,
        "team",
        [((512, D), BF16), ((256, 256), BF16), ((128, 256), BF16), ((64, 256), BF16)],
        [team_rows],
        flops=LONG,
    )(own, got2, got3, got1)
    low4 = exchange(three, 8)
    low6 = exchange(three, 12)
    low2 = exchange(two, 4)
    (block,) = call(collect_kernel, "collect", [((128, 256), BF16)], flops=LONG)(taken)
    got4 = exchange(block, 8)
    got6 = exchange(block, 12)
    got2 = exchange(block, 4)
    (low,) = call(low_kernel, "low", [((256, 256), BF16)], flops=LONG)(low2, low6, low4)

    stacks = ((2, 512, 128), BF16)
    stat = ((2, 1, 512), F32)
    squares = ((2, 768, 512), F32)
    keys, q2, cot2, exps, dweights, top, sums, dots = call(
        first_kernel,
        "first",
        [((2, 768, 256), BF16), stacks, stacks, squares, squares, stat, stat, stat],
        flops=4 * 768 * 1024 * 128,
    )(tokens, one, block, low)
    mids = ((2, 256, 512), F32)
    mid_keys, mid_exps, mid_dweights, top, sums, dots, before = call(
        middle_kernel, "middle", [((256, 256), BF16), mids, mids, stat, stat, stat, stat], flops=4 * 256 * 1024 * 128
    )(got6, got4, q2, cot2, top, sums, dots)
    later = ((2, 640, 512), BF16)
    send2, send4, send6, later_keys, factor, centre, rounded, dscores = call(
        second_kernel,
        "second",
        [((256, 256), BF16), ((192, 256), BF16), ((192, 256), BF16), ((640, 256), BF16), stat, stat, later, later],
        flops=8 * 640 * 1024 * 128,
    )(got2, mid_keys, low, q2, cot2, exps, dweights, mid_exps, mid_dweights, top, sums, dots, before)
    back4 = exchange(send4, 8)
    back6 = exchange(send6, 12)
    back2 = exchange(send2, 4)
    block, one, zero, results = call(
        rest_kernel,
        "rest",
        [((128, 256), F32), ((256, 256), F32), ((512, 256), F32), ((512, 256), BF16)],
        flops=8 * 1152 * 1024 * 128,
    )(keys, later_keys, q2, cot2, exps, dweights, factor, centre, rounded, dscores)

    (back4,) = call(hold_kernel, "hold", [((192, 256), BF16)], flops=LONG)(back4)
    sent, own, near, far = call(
        scatter_kernel,
        "scatter",
        [slots, ((LEAF, 256), F32), whole, ((2 * LEAF, D), BF16)],
        [team_rows, pltpu.VMEM(*slots), pltpu.SemaphoreType.DMA],
        sent_first=True,
    )(block, back2, back4, back6, one, zero, results)
    taken = trade_slots(sent)
    far = exchange(far, 2)
    near = exchange(near, 1)
    (total,) = call(merge_kernel, "merge", [((LEAF, 2 * D), F32)], flops=LONG)(own, near, far)
    (relayed,) = call(relay_kernel, "relay", [whole], after=(total,))(far)
    last = exchange(relayed, 1)
    attended, query_grad = call(outputs_kernel, "outputs", [whole, whole])(results, near, far, last)
    (kv_grad,) = call(finish_kernel, "finish", [((LEAF, 2 * D), BF16)], [pltpu.VMEM((LEAF, 2 * D), F32)])(taken, total, last)
    return attended[None], query_grad[None], kv_grad[None]


def solution(mesh):
    spec = P(None, ("outer", "inner"), None)
    return jax.shard_map(shards, mesh=mesh, in_specs=(spec,) * 3, out_specs=(spec,) * 3, check_vma=False)
```

```python
import functools
import math

import jax
import jax.numpy as jnp
from jax import lax
from jax.experimental import pallas as pl
from jax.experimental.pallas import tpu as pltpu
from jax.sharding import PartitionSpec as P

LEAF = 128
D = 512
TEAM = 4
COLS = 128
HEAD_DIM = 64
LONG = 2 * 10**10
HALF_ROOT = 1.0 / math.sqrt(2.0)
SCALE = 1.0 / math.sqrt(HEAD_DIM)
BF16 = jnp.bfloat16
F32 = jnp.float32
VMEM = pl.BlockSpec(memory_space=pltpu.VMEM)
HBM = pl.BlockSpec(memory_space=pltpu.HBM)
ANYWHERE = pl.BlockSpec(memory_space=pl.ANY)


def call(body, name, outs, scratch=(), flops=0, spec=VMEM, limit=24, after=(), sent_first=False):
    def run(*operands):
        count = len(operands)
        operands = (*operands, *after)
        shapes = [jax.ShapeDtypeStruct(shape, dtype) for shape, dtype in outs]
        moved = sum(math.prod(s.shape) * s.dtype.itemsize for s in (*operands, *shapes))
        return pl.pallas_call(
            (lambda *refs: body(*refs[:count], *refs[count + len(after) :])),
            out_shape=shapes,
            in_specs=[spec] * count + [ANYWHERE] * len(after),
            out_specs=[HBM if sent_first and i == 0 else VMEM for i in range(len(shapes))],
            scratch_shapes=list(scratch),
            name=name,
            cost_estimate=pl.CostEstimate(flops=flops, bytes_accessed=moved, transcendentals=0),
            compiler_params=pltpu.CompilerParams(vmem_limit_bytes=int(limit * 1024 * 1024)),
        )(*operands)

    return run


def exchange(array, bits):
    return lax.ppermute(array, "inner", [(i, i ^ bits) for i in range(16)])


def trade_slots(slots):
    groups = [[16 * o + 4 * team + m for o in range(16) for m in range(TEAM)] for team in range(4)]
    return lax.all_to_all(slots, ("outer", "inner"), 0, 0, axis_index_groups=groups, tiled=True)


def member():
    return lax.axis_index("inner") & 3


def columns(start, group):
    return pl.ds(pl.multiple_of(start + COLS * group, COLS), COLS)


def class_of(k):
    return k.bit_length() - 1


def row_index():
    return lax.broadcasted_iota(jnp.int32, (8, 2 * D), 0)


def read_rows(ref, count, first=0, step=1):
    return jnp.concatenate([ref[c, pl.ds(first, count, stride=step), :] for c in range(ref.shape[0])], axis=1)


def write_rows(ref, rows, first=0, step=1):
    for c in range(ref.shape[0]):
        ref[c, pl.ds(first, rows.shape[0], stride=step), :] = rows[:, 128 * c : 128 * c + 128]


def pool_rows(ref, count):
    pooled = ((read_rows(ref, count // 2, 0, 2) + read_rows(ref, count // 2, 1, 2)) * HALF_ROOT).astype(BF16)
    write_rows(ref, pooled.astype(F32))
    return pooled


def halve(rows, apart):
    pooled = (rows + pltpu.roll(rows, 8 - apart, 0)) * HALF_ROOT
    return pooled.astype(BF16).astype(F32)


def spread(rows, apart):
    row = row_index()
    return rows + jnp.where(row & apart == 0, pltpu.roll(rows, 8 - apart, 0), pltpu.roll(rows, apart, 0))


def pool_kernel(
    q_hbm, kv_hbm, cot_hbm, slots_hbm, own_ref, out1_ref, out2_ref, out3_ref, q_ref, kv_ref, cot_ref, rows_ref, slots_ref, sems
):
    pairs = ((kv_hbm, kv_ref), (q_hbm, q_ref), (cot_hbm, cot_ref))
    copies = [pltpu.make_async_copy(a, b, sems.at[i]) for i, (a, b) in enumerate(pairs)]
    for copy in copies:
        copy.start()
    copies[0].wait()
    write_rows(rows_ref, kv_ref[...].astype(F32))
    for count in (128, 64, 32, 16):
        four = pool_rows(rows_ref, count)
    four = four.astype(F32)
    outer = lax.axis_index("outer")
    row = row_index()
    five = halve(four, 1)
    six = halve(five, 2)
    seven = halve(six, 4)
    five = jnp.where(row & 1 == 0, five, pltpu.roll(five, 1, 0))
    six = spread(spread(jnp.where(row & 3 == 0, six, 0.0), 1), 2)
    seven = jnp.broadcast_to(seven[:1], seven.shape)
    table = [
        four,
        jnp.where(row & 1 == outer & 1, five, 0.0),
        jnp.where(row & 3 == outer & 3, six, 0.0),
        jnp.where(row == outer & 7, seven, 0.0),
    ]
    for m in range(TEAM):
        keys, values = slice(COLS * m, COLS * m + COLS), slice(D + COLS * m, D + COLS * m + COLS)
        blocks = [jnp.concatenate([rows[:, keys], rows[:, values]], axis=0).astype(BF16) for rows in table]
        slots_ref[outer * TEAM + m] = jnp.zeros_like(blocks[0])
        for k in range(1, 16):
            slots_ref[(outer ^ k) * TEAM + m] = blocks[class_of(k)]
    sent = pltpu.make_async_copy(slots_ref, slots_hbm, sems.at[3])
    sent.start()
    copies[1].wait()
    copies[2].wait()
    for k, ref in enumerate((own_ref, out1_ref, out2_ref, out3_ref)):
        group = member() ^ k
        ref[:, 0:128] = q_ref[:, columns(0, group)]
        ref[:, 128:256] = kv_ref[:, columns(0, group)]
        ref[:, 256:384] = kv_ref[:, columns(D, group)]
        ref[:, 384:512] = cot_ref[:, columns(0, group)]
    sent.wait()


def class_sums(slots_ref):
    outer = lax.axis_index("outer")

    def total(c, m):
        return functools.reduce(jnp.add, [slots_ref[(outer ^ k) * TEAM + m].astype(F32) for k in range(1 << c, 2 << c)])

    return [[total(c, m) for m in range(TEAM)] for c in range(4)]


def side_by_side(block):
    return jnp.concatenate([block[:8], block[8:]], axis=1)


def team_kernel(own_ref, got2_ref, got3_ref, got1_ref, tokens_ref, one_ref, two_ref, three_ref, rows_ref):
    for k, ref in enumerate((own_ref, got1_ref, got2_ref, got3_ref)):
        tokens_ref[LEAF * k : LEAF * k + LEAF, :] = ref[...]
    write_rows(rows_ref, tokens_ref[:, 128:384].astype(F32))
    one_ref[...] = pool_rows(rows_ref, 512)
    two_ref[...] = pool_rows(rows_ref, 256)
    three_ref[...] = pool_rows(rows_ref, 128)


def collect_kernel(slots_ref, block_ref):
    block_ref[...] = jnp.concatenate(
        [side_by_side(b) for blocks in class_sums(slots_ref) for b in blocks], axis=0
    ).astype(BF16)


def low_kernel(two_ref, six_ref, four_ref, out_ref):
    out_ref[0:128, :] = two_ref[...]
    out_ref[128:192, :] = four_ref[...]
    out_ref[192:256, :] = six_ref[...]


def across(a, b):
    return lax.dot_general(a, b, (((1,), (1,)), ((), ())), preferred_element_type=F32)


def along(a, b):
    return lax.dot_general(a, b, (((0,), (0,)), ((), ())), preferred_element_type=F32)


def two_heads(block):
    low_half = lax.broadcasted_iota(jnp.int32, block.shape, 1) < HEAD_DIM
    return jnp.concatenate([jnp.where(low_half, block, 0.0), jnp.where(low_half, 0.0, block)], axis=0).astype(BF16)


def first_kernel(
    tokens_ref, one_ref, block_ref, low_ref, keys_ref, q2_ref, cot2_ref, exps_ref, dweights_ref, max_ref, sum_ref, dot_ref
):
    for s in range(2):
        tokens = slice(256 * s, 256 * s + 256)
        keys_ref[s, 0:256, :] = tokens_ref[tokens, 128:384]
        keys_ref[s, 256:384, :] = one_ref[128 - 128 * s : 256 - 128 * s, :]
        keys_ref[s, 384:512, :] = block_ref[...]
        keys_ref[s, 512:768, :] = low_ref[...]
        queries = two_heads(tokens_ref[tokens, 0:128].astype(F32) * SCALE)
        grads = two_heads(tokens_ref[tokens, 384:512].astype(F32))
        q2_ref[s] = queries
        cot2_ref[s] = grads
        scores = across(keys_ref[s, :, 0:128], queries)
        top = jnp.max(scores, axis=0, keepdims=True)
        exps = jnp.exp(scores - top)
        dweights = across(keys_ref[s, :, 128:256], grads)
        exps_ref[s] = exps
        dweights_ref[s] = dweights
        max_ref[s] = top
        sum_ref[s] = jnp.sum(exps, axis=0, keepdims=True)
        dot_ref[s] = jnp.sum(exps * dweights, axis=0, keepdims=True)


def middle_kernel(
    got6_ref, got4_ref, q2_ref, cot2_ref, max_ref, sum_ref, dot_ref,
    keys_ref, exps_ref, dweights_ref, top_ref, total_ref, dots_ref, before_ref,
):
    keys_ref[0:128, :] = got4_ref[...]
    keys_ref[128:256, :] = got6_ref[...]
    for s in range(2):
        scores = across(keys_ref[:, 0:128], q2_ref[s])
        dweights = across(keys_ref[:, 128:256], cot2_ref[s])
        top = jnp.maximum(max_ref[s], jnp.max(scores, axis=0, keepdims=True))
        exps = jnp.exp(scores - top)
        before = jnp.exp(max_ref[s] - top)
        exps_ref[s] = exps
        dweights_ref[s] = dweights
        top_ref[s] = top
        total_ref[s] = sum_ref[s] * before + jnp.sum(exps, axis=0, keepdims=True)
        dots_ref[s] = dot_ref[s] * before + jnp.sum(exps * dweights, axis=0, keepdims=True)
        before_ref[s] = before


def second_kernel(
    got2_ref, mid_ref, low_ref, q2_ref, cot2_ref, exps_ref, dweights_ref, mid_exps_ref, mid_dweights_ref, max_ref, sum_ref, dot_ref, first_ref,
    send2_ref, send4_ref, send6_ref, keys_ref, factor_ref, centre_ref, rounded_ref, dscores_ref,
):
    keys_ref[0:128, :] = got2_ref[...]
    keys_ref[128:384, :] = mid_ref[...]
    keys_ref[384:640, :] = low_ref[...]
    dkeys, dvals = [], []
    for s in range(2):
        queries, grads = q2_ref[s], cot2_ref[s]
        scores = across(keys_ref[0:128, 0:128], queries)
        dweights = across(keys_ref[0:128, 128:256], grads)
        top = jnp.maximum(max_ref[s], jnp.max(scores, axis=0, keepdims=True))
        exps = jnp.exp(scores - top)
        before = jnp.exp(max_ref[s] - top)
        inverse = 1.0 / (sum_ref[s] * before + jnp.sum(exps, axis=0, keepdims=True))
        centre = (dot_ref[s] * before + jnp.sum(exps * dweights, axis=0, keepdims=True)) * inverse
        middle = before * inverse
        factor = first_ref[s] * middle
        weights = jnp.concatenate([exps * inverse, mid_exps_ref[s] * middle, exps_ref[s, 512:768, :] * factor], axis=0)
        dweights = jnp.concatenate([dweights, mid_dweights_ref[s], dweights_ref[s, 512:768, :]], axis=0)
        rounded = weights.astype(BF16)
        dscores = (weights * (dweights - centre)).astype(BF16)
        factor_ref[s] = factor
        centre_ref[s] = centre
        rounded_ref[s] = rounded
        dscores_ref[s] = dscores
        dkeys.append(jnp.dot(dscores, queries, preferred_element_type=F32))
        dvals.append(jnp.dot(rounded, grads, preferred_element_type=F32))
    for cols, parts in ((slice(0, 128), dkeys), (slice(128, 256), dvals)):
        total = (parts[0] + parts[1]).astype(BF16)
        send2_ref[0:128, cols] = total[0:128]
        send2_ref[128:256, cols] = total[384:512]
        send4_ref[0:128, cols] = total[128:256]
        send4_ref[128:192, cols] = total[512:576]
        send6_ref[0:128, cols] = total[256:384]
        send6_ref[128:192, cols] = total[576:640]


def rest_kernel(
    keys_ref, later_ref, q2_ref, cot2_ref, exps_ref, dweights_ref, factor_ref, centre_ref, rounded_ref, dscores_ref,
    block_ref, one_ref, zero_ref, results_ref,
):
    totals = []
    for s in range(2):
        weights = exps_ref[s, 0:512, :] * factor_ref[s]
        rounded = weights.astype(BF16)
        dscores = (weights * (dweights_ref[s, 0:512, :] - centre_ref[s])).astype(BF16)
        dkeys = jnp.dot(dscores, q2_ref[s], preferred_element_type=F32)
        dvals = jnp.dot(rounded, cot2_ref[s], preferred_element_type=F32)
        total = jnp.concatenate([dkeys, dvals], axis=1)
        zero_ref[256 * s : 256 * s + 256, :] = total[0:256]
        one_ref[128 - 128 * s : 256 - 128 * s, :] = total[256:384]
        totals.append(total[384:512])
        attended = along(keys_ref[s, 0:512, 128:256], rounded) + along(later_ref[:, 128:256], rounded_ref[s])
        query_grad = along(keys_ref[s, 0:512, 0:128], dscores) + along(later_ref[:, 0:128], dscores_ref[s])
        for i in range(2):
            rows = slice(256 * s + LEAF * i, 256 * s + LEAF * i + LEAF)
            low, high = slice(LEAF * i, LEAF * i + LEAF), slice(256 + LEAF * i, 256 + LEAF * i + LEAF)
            for cols, pair, scale in ((slice(0, 128), attended, 1.0), (slice(128, 256), query_grad, SCALE)):
                mine = jnp.concatenate([pair[:HEAD_DIM, low], pair[HEAD_DIM:, high]], axis=0).T
                results_ref[rows, cols] = (mine * scale).astype(BF16)
    block_ref[...] = totals[0] + totals[1]


def add(*parts):
    return functools.reduce(jnp.add, [p.astype(F32) for p in parts])


def four_kernel(block_ref, got_ref, out_ref):
    out_ref[0:128, :] = add(block_ref[...], got_ref[0:128, :])
    out_ref[128:192, :] = got_ref[128:192, :].astype(F32)


def scatter_kernel(
    back2_ref, back4_ref, back6_ref, one_ref, zero_ref, results_ref,
    slots_hbm, own_ref, near_ref, far_ref, rows_ref, slots_ref, sem,
):
    outer = lax.axis_index("outer")
    total = add(back2_ref[0:128, :], back4_ref[0:128, :], back6_ref[0:128, :])
    for m in range(TEAM):
        slots_ref[outer * TEAM + m] = jnp.zeros((16, COLS), BF16)
        for c in range(4):
            rows = total[32 * c + 8 * m : 32 * c + 8 * m + 8]
            block = jnp.concatenate([rows[:, :COLS], rows[:, COLS:]], axis=0).astype(BF16)
            for k in range(1 << c, 2 << c):
                slots_ref[(outer ^ k) * TEAM + m] = block
    sent = pltpu.make_async_copy(slots_ref, slots_hbm, sem)
    sent.start()
    total = add(back4_ref[128:192, :], back6_ref[128:192, :])
    count = 64
    for level in (back2_ref[128:256, :], one_ref[...], zero_ref[...]):
        write_rows(rows_ref, total, 0, 2)
        write_rows(rows_ref, total, 1, 2)
        count *= 2
        total = level.astype(F32) + HALF_ROOT * read_rows(rows_ref, count)
    own_ref[...] = total[0:LEAF]
    for k, ref in enumerate((near_ref, far_ref.at[0:LEAF, :], far_ref.at[LEAF : 2 * LEAF, :])):
        rows = slice(LEAF * (k + 1), LEAF * (k + 2))
        ref[:, 0:256] = total[rows].astype(BF16)
        ref[:, 256:512] = results_ref[rows, :]
    sent.wait()


def merge_kernel(own_ref, near_ref, far_ref, sum_ref):
    for k, ref in enumerate((own_ref, near_ref, far_ref)):
        sum_ref[:, columns(0, member() ^ k)] = ref[0:LEAF, 0:128].astype(F32)
        sum_ref[:, columns(D, member() ^ k)] = ref[0:LEAF, 128:256].astype(F32)


def relay_kernel(far_ref, out_ref):
    out_ref[...] = far_ref[LEAF : 2 * LEAF, :]


def outputs_kernel(results_ref, near_ref, far_ref, last_ref, att_ref, dq_ref):
    parts = [results_ref[0:LEAF, :]] + [ref[0:LEAF, 256:512] for ref in (near_ref, far_ref, last_ref)]
    for k, part in enumerate(parts):
        att_ref[:, columns(0, member() ^ k)] = part[:, :COLS]
        dq_ref[:, columns(0, member() ^ k)] = part[:, COLS:]


def finish_kernel(slots_ref, sum_in_ref, last_ref, out_ref, sum_ref):
    sum_ref[...] = sum_in_ref[...]
    sum_ref[:, columns(0, member() ^ 3)] = last_ref[:, 0:128].astype(F32)
    sum_ref[:, columns(D, member() ^ 3)] = last_ref[:, 128:256].astype(F32)
    outer = lax.axis_index("outer")
    row = row_index()
    four, five, six, seven = [
        jnp.concatenate([b[:8] for b in blocks] + [b[8:] for b in blocks], axis=1) for blocks in class_sums(slots_ref)
    ]
    five = spread(jnp.where(row & 1 == outer & 1, five, 0.0), 1)
    six = spread(spread(jnp.where(row & 3 == outer & 3, six, 0.0), 1), 2)
    seven = jnp.sum(jnp.where(row == outer & 7, seven, 0.0), axis=0, keepdims=True)
    total = four + HALF_ROOT * (five + HALF_ROOT * (six + HALF_ROOT * seven))
    total = total * 0.25
    for r in range(8):
        rows = slice(16 * r, 16 * r + 16)
        out_ref[rows, :] = (sum_ref[rows, :] + total[r : r + 1]).astype(BF16)


def shards(queries, keys_values, cotangent):
    queries, keys_values, cotangent = queries[0], keys_values[0], cotangent[0]
    whole = ((LEAF, D), BF16)
    slots = ((16 * TEAM, 16, COLS), BF16)
    piece = ((LEAF, D), BF16)
    loaded = [pltpu.VMEM((LEAF, D), BF16), pltpu.VMEM((LEAF, 2 * D), BF16), pltpu.VMEM((LEAF, D), BF16)]
    own_rows = pltpu.VMEM((8, LEAF, 128), F32)
    team_rows = pltpu.VMEM((2, TEAM * LEAF, 128), F32)

    sent, own, out1, out2, out3 = call(
        pool_kernel, "pool", [slots, piece, piece, piece, piece], [*loaded, own_rows, pltpu.VMEM(*slots), pltpu.SemaphoreType.DMA((4,))], spec=HBM, limit=53.375, sent_first=True
    )(queries, keys_values, cotangent)
    taken = trade_slots(sent)
    got2 = exchange(out2, 2)
    got3 = exchange(out3, 3)
    got1 = exchange(out1, 1)
    tokens, one, two, three = call(
        team_kernel,
        "team",
        [((512, D), BF16), ((256, 256), BF16), ((128, 256), BF16), ((64, 256), BF16)],
        [team_rows],
        flops=LONG,
    )(own, got2, got3, got1)
    low4 = exchange(three, 8)
    low6 = exchange(three, 12)
    low2 = exchange(two, 4)
    (block,) = call(collect_kernel, "collect", [((128, 256), BF16)], flops=LONG)(taken)
    got4 = exchange(block, 8)
    got6 = exchange(block, 12)
    got2 = exchange(block, 4)
    (low,) = call(low_kernel, "low", [((256, 256), BF16)], flops=LONG)(low2, low6, low4)

    stacks = ((2, 512, 128), BF16)
    stat = ((2, 1, 512), F32)
    squares = ((2, 768, 512), F32)
    keys, q2, cot2, exps, dweights, top, sums, dots = call(
        first_kernel,
        "first",
        [((2, 768, 256), BF16), stacks, stacks, squares, squares, stat, stat, stat],
        flops=4 * 768 * 1024 * 128,
    )(tokens, one, block, low)
    mids = ((2, 256, 512), F32)
    mid_keys, mid_exps, mid_dweights, top, sums, dots, before = call(
        middle_kernel, "middle", [((256, 256), BF16), mids, mids, stat, stat, stat, stat], flops=4 * 256 * 1024 * 128
    )(got6, got4, q2, cot2, top, sums, dots)
    later = ((2, 640, 512), BF16)
    send2, send4, send6, later_keys, factor, centre, rounded, dscores = call(
        second_kernel,
        "second",
        [((256, 256), BF16), ((192, 256), BF16), ((192, 256), BF16), ((640, 256), BF16), stat, stat, later, later],
        flops=8 * 640 * 1024 * 128,
    )(got2, mid_keys, low, q2, cot2, exps, dweights, mid_exps, mid_dweights, top, sums, dots, before)
    back4 = exchange(send4, 8)
    back6 = exchange(send6, 12)
    back2 = exchange(send2, 4)
    block, one, zero, results = call(
        rest_kernel,
        "rest",
        [((128, 256), F32), ((256, 256), F32), ((512, 256), F32), ((512, 256), BF16)],
        flops=8 * 1152 * 1024 * 128,
    )(keys, later_keys, q2, cot2, exps, dweights, factor, centre, rounded, dscores)

    (back4,) = call(four_kernel, "four", [((192, 256), F32)], flops=LONG)(block, back4)
    sent, own, near, far = call(
        scatter_kernel,
        "scatter",
        [slots, ((LEAF, 256), F32), whole, ((2 * LEAF, D), BF16)],
        [team_rows, pltpu.VMEM(*slots), pltpu.SemaphoreType.DMA],
        sent_first=True,
    )(back2, back4, back6, one, zero, results)
    taken = trade_slots(sent)
    far = exchange(far, 2)
    near = exchange(near, 1)
    (total,) = call(merge_kernel, "merge", [((LEAF, 2 * D), F32)], flops=LONG)(own, near, far)
    (relayed,) = call(relay_kernel, "relay", [whole], after=(total,))(far)
    last = exchange(relayed, 1)
    attended, query_grad = call(outputs_kernel, "outputs", [whole, whole])(results, near, far, last)
    (kv_grad,) = call(finish_kernel, "finish", [((LEAF, 2 * D), BF16)], [pltpu.VMEM((LEAF, 2 * D), F32)])(taken, total, last)
    return attended[None], query_grad[None], kv_grad[None]


def solution(mesh):
    spec = P(None, ("outer", "inner"), None)
    return jax.shard_map(shards, mesh=mesh, in_specs=(spec,) * 3, out_specs=(spec,) * 3, check_vma=False)
```
